512 devices in a mesh: row: 8 (over z), au: 8 (over y), vert: 8 (over x, core).
Axes of the slice: x: 4, y: 8, z: 8, core: 2. Of those that a mesh axis runs over, the one named last changes fastest.
Arguments:
- velocity: float32 [32, 128, 2048], P('row', 'au', 'vert'), may hold values from -6 to 6
- log_visc: float32 [32, 128, 2048], P('row', 'au', 'vert'), may hold values from -3.45 to 3.45
- labels: int32 [128, 2048], P('au', 'vert'), may hold values from 0 to 511
- seg_dir: float32 [512], replicated, may hold values from -5 to 5
- layer_dir: float32 [32], P('row'), may hold values from -5 to 5
Outputs:
- increment: float32 [32, 128, 2048], P('row', 'au', 'vert')
- adjoint: float32 [32, 128, 2048], P('row', 'au', 'vert')
- hv_segments: float32 [512], replicated
- hv_layers: float32 [32], P('row')
The draws below stay inside these ranges and needn't reach their ends.
All inputs are finite; a program needn't handle non-finite values.
Results may differ from the reference program's by a relative error of at most 0.000022.
Values sent between devices are 32-bit elements; how exact they have to be, the bound alone decides.
No kernel may reach another device: no remote copies, remote signals or barrier semaphores. Data moves between devices by JAX's collectives and lax.ppermute only.
A program may use at most 64 MiB of HBM per device.

```python
import jax
import jax.numpy as jnp

NSEG = 512
SWEEPS = 2
COARSE_SWEEPS = 4
NR = 32
NA = 128
NV = 2048


def set_ends(values, rng, smallest, largest):
    longest = values.shape.index(max(values.shape))
    spots = []
    for shift in (0, 1):
        where = [jax.random.randint(jax.random.fold_in(rng, axis), (), 0, length) for axis, length in enumerate(values.shape)]
        where[longest] = (where[longest] + shift) % values.shape[longest]
        spots.append(tuple(where))
    return values.at[spots[0]].set(smallest).at[spots[1]].set(largest)


def steps_of(own_key, shape, cuts, smallest, largest):
    level = 1.0
    for dim, parts in cuts:
        draws = jax.random.uniform(jax.random.fold_in(jax.random.fold_in(own_key, 6), dim), (parts,), jnp.float32, smallest / len(cuts), largest / len(cuts))
        level = level * jnp.repeat(jnp.exp(draws), shape[dim] // parts).reshape((-1,) + (1,) * (len(shape) - 1 - dim))
    return level


def noise(rng, dims, spread, bound, pieces=(), kind=jnp.bfloat16):
    drawn = spread * jax.random.normal(rng, dims, jnp.float32)
    if pieces:
        drawn = drawn * steps_of(rng, dims, pieces, -0.22, 0.18)
    return jnp.clip(drawn, -bound, bound).astype(kind)


def setup_inputs(seed: int = 0) -> dict:
    splits = jax.random.split(jax.random.key(seed), 6)
    velocity = noise(splits[0], (NR, NA, NV), 1.0, 6.0, ((0, 8), (1, 8), (2, 8)), jnp.float32)
    log_visc = jnp.clip(jax.random.uniform(splits[1], (NR, NA, NV), jnp.float32, -3.45, 3.45) * steps_of(splits[1], (NR, NA, NV), ((0, 8), (1, 8), (2, 8)), -0.4, 0.0), -3.45, 3.45)
    labels = set_ends(jax.random.randint(splits[2], (NA, NV), 0, NSEG), jax.random.fold_in(splits[2], 1), 0, NSEG - 1).astype(jnp.int32)
    seg_dir = noise(splits[3], (NSEG,), 1.0, 5.0, (), jnp.float32)
    layer_dir = noise(splits[4], (NR,), 1.0, 5.0, ((0, 8),), jnp.float32)
    return {"velocity": velocity, "log_visc": log_visc, "labels": labels, "seg_dir": seg_dir, "layer_dir": layer_dir}


DAMPING = 0.7
COARSE_FACTOR = 0.25
DIRECTIONS = ((0, -1), (0, 1), (1, -1), (1, 1), (2, -1), (2, 1))


def neighbor(padded, dim_no, offset):
    slicers = [slice(1, -1), slice(1, -1), slice(1, -1)]
    slicers[dim_no] = slice(1 + offset, padded.shape[dim_no] - 1 + offset)
    return padded[tuple(slicers)]


def centre(padded):
    return padded[1:-1, 1:-1, 1:-1]


def inside_masks(extent, starts, totals):
    result = []
    for dim_no, offset in DIRECTIONS:
        global_at = starts[dim_no] + jnp.arange(extent[dim_no], dtype=jnp.int32) + offset
        inside = (global_at >= 0) & (global_at < totals[dim_no])
        layout = [1, 1, 1]
        layout[dim_no] = extent[dim_no]
        result.append(jnp.broadcast_to(inside.reshape(layout), tuple(extent)))
    return result


def face_weights(log_padded, masks_list, factor):
    middle = centre(log_padded)
    weights = []
    for number in range(6):
        dim_no, offset = DIRECTIONS[number]
        beside = neighbor(log_padded, dim_no, offset)
        weights.append(factor * jnp.where(masks_list[number], jnp.exp(0.5 * (middle + beside)), jnp.exp(middle)))
    return weights


def diagonal_of(weights):
    result = weights[0]
    for number in range(1, 6):
        result = result + weights[number]
    return result


def apply_operator(padded, weights):
    middle = centre(padded)
    result = weights[0] * (middle - neighbor(padded, 0, -1))
    for number in range(1, 6):
        dim_no, offset = DIRECTIONS[number]
        result = result + weights[number] * (middle - neighbor(padded, dim_no, offset))
    return result


def restrict(values):
    shaped = values.reshape(values.shape[0] // 2, 2, values.shape[1] // 2, 2, values.shape[2] // 2, 2)
    return jnp.sum(shaped, axis=(1, 3, 5)) * 0.125


def prolong(values):
    return jnp.repeat(jnp.repeat(jnp.repeat(values, 2, axis=0), 2, axis=1), 2, axis=2)


def jacobi(iterate, source, level):
    weights, diag_sum, pad_fn = level
    applied = apply_operator(pad_fn(iterate), weights)
    return iterate + DAMPING * (source - applied) / diag_sum


def vcycle(source, fine_level, coarse_level, to_coarse, from_coarse):
    iterate = jnp.zeros_like(source)
    for sweep_no in range(SWEEPS):
        iterate = jacobi(iterate, source, fine_level)
    leftover = source - apply_operator(fine_level[2](iterate), fine_level[0])
    coarse_source = to_coarse(restrict(leftover))
    correction = jnp.zeros_like(coarse_source)
    for sweep_no in range(COARSE_SWEEPS):
        correction = jacobi(correction, coarse_source, coarse_level)
    iterate = iterate + prolong(from_coarse(correction))
    for sweep_no in range(SWEEPS):
        iterate = jacobi(iterate, source, fine_level)
    return iterate


def depth_weight(row_ids, total_rows):
    return jnp.exp(-(total_rows - 1 - row_ids).astype(jnp.float32) / (total_rows / 4.0))


def forcing_term(vel_padded, step_padded, weights, masks_list):
    middle = centre(vel_padded)
    step_mid = centre(step_padded)
    result = jnp.zeros_like(middle)
    for number in range(6):
        dim_no, offset = DIRECTIONS[number]
        step_face = jnp.where(masks_list[number], 0.5 * (step_mid + neighbor(step_padded, dim_no, offset)), step_mid)
        result = result - weights[number] * step_face * (middle - neighbor(vel_padded, dim_no, offset))
    return result


def density_term(vel_padded, adj_padded, weights, masks_list):
    vel_mid = centre(vel_padded)
    adj_mid = centre(adj_padded)
    result = jnp.zeros_like(vel_mid)
    for number in range(6):
        dim_no, offset = DIRECTIONS[number]
        halves = jnp.where(masks_list[number], 0.5, 1.0)
        result = result + halves * weights[number] * (neighbor(adj_padded, dim_no, offset) - adj_mid) * (neighbor(vel_padded, dim_no, offset) - vel_mid)
    return result


def zero_pad(values):
    return jnp.pad(values, 1)


def keep_same(values):
    return values


def reference(velocity, log_visc, labels, seg_dir, layer_dir):
    row_ids = jnp.arange(NR, dtype=jnp.int32)
    depth_scale = depth_weight(row_ids, NR)
    log_step = seg_dir[labels][None, :, :] * depth_scale[:, None, None] + layer_dir[:, None, None]
    extent = (NR, NA, NV)
    masks_list = inside_masks(extent, (0, 0, 0), extent)
    weights = face_weights(zero_pad(log_visc), masks_list, 1.0)
    fine_level = (weights, diagonal_of(weights), zero_pad)
    coarse_extent = (NR // 2, NA // 2, NV // 2)
    coarse_masks = inside_masks(coarse_extent, (0, 0, 0), coarse_extent)
    coarse_weights = face_weights(zero_pad(restrict(log_visc)), coarse_masks, COARSE_FACTOR)
    coarse_level = (coarse_weights, diagonal_of(coarse_weights), zero_pad)
    vel_padded = zero_pad(velocity)
    source = forcing_term(vel_padded, zero_pad(log_step), weights, masks_list)
    increment = vcycle(source, fine_level, coarse_level, keep_same, keep_same)
    adjoint = vcycle(-increment, fine_level, coarse_level, keep_same, keep_same)
    density = density_term(vel_padded, zero_pad(adjoint), weights, masks_list)
    column = jnp.sum(depth_scale[:, None, None] * density, axis=0)
    seg_total = jax.ops.segment_sum(column.reshape(-1), labels.reshape(-1), num_segments=NSEG)
    layer_total = jnp.sum(density, axis=(1, 2))
    seg_scale = 1.0 / (NR * NA * NV / NSEG) ** 0.5
    layer_scale = 1.0 / (NA * NV) ** 0.5
    return increment, adjoint, seg_total * seg_scale, layer_total * layer_scale
```

```python
import jax
import jax.numpy as jnp
from jax import lax
from jax.experimental import pallas as pl
from jax.experimental.pallas import tpu as pltpu
from jax.sharding import PartitionSpec as P

NSEG = 512
DAMPING = 0.7
KEEP = 1.0 - DAMPING
COARSE_FACTOR = 0.25

LAYERS = 32
OWN = 16
HALO = 12
WINDOW = OWN + 2 * HALO
PART = 32
MARGIN = 24
SPAN = PART + 2 * MARGIN
LANES = 128
TOP = 8
PAD_ROWS = WINDOW + 2 * TOP
TILES = 40
F32 = jnp.float32
VMEM_LIMIT = 48 * 1024 * 1024


def lanes_of(shape):
    return lax.broadcasted_iota(jnp.int32, shape, len(shape) - 1)


def turn(values, amount):
    return pltpu.roll(values, amount % LANES, values.ndim - 1)


def call(kernel, outs, scratch=()):
    return pl.pallas_call(
        kernel,
        out_shape=outs,
        scratch_shapes=list(scratch),
        compiler_params=pltpu.CompilerParams(vmem_limit_bytes=VMEM_LIMIT),
    )


def sds(*shape):
    return jax.ShapeDtypeStruct(shape, F32)


def edge_kernel(vel, log, lab, seg, left, right, plate):
    for top in (0, 8):
        for half in range(2):
            labels = lab[top : top + 8, half * LANES : (half + 1) * LANES]
            low = labels & 127
            high = labels >> 7
            value = jnp.zeros((8, LANES), F32)
            for part in range(4):
                table = jnp.broadcast_to(seg[part : part + 1, :], (8, LANES))
                got = jnp.take_along_axis(table, low, axis=1, mode="promise_in_bounds")
                value = jnp.where(high == part, got, value)
            plate[top : top + 8, half * LANES : (half + 1) * LANES] = value
    slot = lanes_of((OWN, LANES)) // PART
    for group, field in enumerate((vel, log)):
        first = field[0, :, 0:LANES]
        last = turn(field[0, :, LANES : 2 * LANES], MARGIN)
        for row in range(1, 4):
            first = jnp.where(slot == row, turn(field[row, :, 0:LANES], PART * row), first)
            last = jnp.where(slot == row, turn(field[row, :, LANES : 2 * LANES], PART * row + MARGIN), last)
        left[group] = first
        right[group] = last
    left[2] = plate[:, 0:LANES]
    right[2] = turn(plate[:, LANES : 2 * LANES], MARGIN)


def stretched(first, second, before, after, row):
    lane = lanes_of(first.shape)
    head = lane < MARGIN
    first = turn(first, MARGIN)
    second = turn(second, MARGIN)
    return (
        jnp.where(head, turn(before, -PART * row), first),
        jnp.where(head, first, second),
        jnp.where(head, second, turn(after, MARGIN - PART * row)),
    )


def window_kernel(vel, log, lab, plate, before, after, layer, send, plate_window, label_window):
    lane = lanes_of((OWN, LANES))
    for group, field in enumerate((vel, log)):
        for row in range(4):
            slab = group * 4 + row
            tiles = stretched(
                field[row, :, 0:LANES], field[row, :, LANES : 2 * LANES], before[group], after[group], row
            )
            for part in range(8):
                base, shift = part // 4, PART * (part % 4)
                if shift:
                    wide = jnp.where(
                        lane < LANES - shift, turn(tiles[base], -shift), turn(tiles[base + 1], -shift)
                    )
                else:
                    wide = tiles[base]
                if group == 0:
                    wide = jnp.where(lane == SPAN - 1, layer[row], wide)
                start = 64 * (slab % 2)
                send[part, slab // 2, :, start : start + 64] = wide[:, 0:64]
                send[part, 4, :, 16 * slab : 16 * slab + 16] = wide[:, 64:80]
    part = lax.axis_index("row")
    shift = PART * (part % 4)
    tiles = stretched(plate[:, 0:LANES], plate[:, LANES : 2 * LANES], before[2], after[2], 0)
    late = part >= 4
    here = jnp.where(late, tiles[1], tiles[0])
    there = jnp.where(late, tiles[2], tiles[1])
    back = (LANES - shift) % LANES
    plate_window[...] = jnp.where(lane < LANES - shift, pltpu.roll(here, back, 1), pltpu.roll(there, back, 1))
    labels = jnp.where(late, lab[:, LANES : 2 * LANES], lab[:, 0:LANES])
    label_window[...] = pltpu.roll(labels, (LANES + MARGIN - shift) % LANES, 1)


def rows_kernel(got, plate_window, up, down):
    def tile(index):
        if index < TILES:
            return got[index // 5, index % 5]
        return plate_window[...]

    for index in range(TILES + 1):
        values = tile(index)
        at = TILES + 1 + index // 2
        half = 4 * (index % 2)
        up[index] = values[8:16]
        down[index] = values[0:8]
        up[at, half : half + 4, :] = values[4:8]
        down[at, half : half + 4, :] = values[8:12]


def rows_of(index, up, down, total):
    at = total + index // 2
    half = 4 * (index % 2)
    return up[at, half : half + 4, :], up[index], down[index], down[at, half : half + 4, :]


def places():
    row_at = lax.broadcasted_iota(jnp.int32, (WINDOW, LANES), 0)
    lane = lanes_of((WINDOW, LANES))
    across = row_at + (lax.axis_index("au") * OWN - HALO)
    along = lane + (lax.axis_index("vert") * (8 * PART) + lax.axis_index("row") * PART - MARGIN)
    across_end = lax.axis_size("au") * OWN
    along_end = lax.axis_size("vert") * 8 * PART
    domain = (across >= 0) & (across < across_end) & (along >= 0) & (along < along_end) & (lane < SPAN)
    return row_at, lane, across, along, across_end, along_end, domain


def middle(ref, at):
    return ref[at, TOP : TOP + WINDOW, :]


def four(ref, at, reach=1):
    centre = middle(ref, at)
    return (
        centre,
        ref[at, TOP - reach : TOP - reach + WINDOW, :],
        ref[at, TOP + reach : TOP + reach + WINDOW, :],
        turn(centre, reach),
        turn(centre, -reach),
    )


def around(ref, at, reach=1):
    centre, low, high, left, right = four(ref, at, reach)
    total = (low + high) + (left + right)
    return centre, total + (middle(ref, at - 1) + middle(ref, at + 1))


def pair_sum(values, even_row, even_lane):
    shaped = values.reshape(WINDOW // 8, 8, LANES)
    partner = jnp.where(even_row, pltpu.roll(shaped, 7, 1), pltpu.roll(shaped, 1, 1))
    shaped = shaped + partner
    partner = jnp.where(even_lane, turn(shaped, -1), turn(shaped, 1))
    return (shaped + partner).reshape(WINDOW, LANES)


def parities():
    shape = (WINDOW // 8, 8, LANES)
    return lax.broadcasted_iota(jnp.int32, shape, 1) % 2 == 0, lanes_of(shape) % 2 == 0


def clear_edges(refs):
    for ref in refs:
        last = ref.shape[0] - 1
        zero = jnp.zeros((TOP, LANES), F32)
        zeros = jnp.zeros((PAD_ROWS, LANES), F32)
        ref[0] = zeros
        ref[last] = zeros

        def clear(at, _, ref=ref, zero=zero):
            ref[at, 0:TOP, :] = zero
            ref[at, TOP + WINDOW : PAD_ROWS, :] = zero
            return 0

        lax.fori_loop(1, last, clear, 0)


def loop(count, body, unroll=2):
    def step(at, _):
        body(at)
        return 0

    lax.fori_loop(0, count, step, 0, unroll=unroll)


def smooth(out, values, source, factor, count, reach, first=False):
    def body(at):
        centre, total = around(values, at + 1, reach)
        if first:
            out[at + 1, TOP : TOP + WINDOW, :] = (1.0 + KEEP) * centre + factor[at] * total
        else:
            out[at + 1, TOP : TOP + WINDOW, :] = (
                KEEP * centre + middle(source, at + 1) + factor[at] * total
            )

    loop(count, body)


def vcycle(f, one, two, zf, za, zb, g, c, big, cc, kc, ginv):
    even_row, even_lane = parities()
    smooth(two, f, None, c, LAYERS, 1, first=True)

    def leftover(at):
        centre, total = around(two, at + 1)
        return big[at] * ((middle(f, at + 1) - DAMPING * centre) + c[at] * total)

    def down(at):
        total = leftover(2 * at) + leftover(2 * at + 1)
        zf[at + 1, TOP : TOP + WINDOW, :] = kc[at] * pair_sum(total, even_row, even_lane)

    loop(LAYERS // 2, down, 1)
    smooth(za, zf, None, cc, LAYERS // 2, 2, first=True)
    smooth(zb, za, zf, cc, LAYERS // 2, 2)
    smooth(za, zb, zf, cc, LAYERS // 2, 2)

    def up(at):
        value = middle(za, at + 1) * ginv[at]
        for row in range(2):
            one[2 * at + row + 1, TOP : TOP + WINDOW, :] = (
                middle(two, 2 * at + row + 1) + middle(g, 2 * at + row + 1) * value
            )

    loop(LAYERS // 2, up)
    smooth(two, one, f, c, LAYERS, 1)
    smooth(one, two, f, c, LAYERS, 1)


def depth_at(at):
    place = jnp.zeros((8, LANES), jnp.int32) + at
    return jnp.exp(-(LAYERS - 1 - place).astype(F32) / (LAYERS / 4.0))


def tall(values):
    return jnp.concatenate([values] * (WINDOW // 8), axis=0)


def first_kernel(
    got, plate_window, from_low, from_high,
    g, c, big, cc, kc, ginv, vel, f_own, f_up, f_down, inc,
    packed, f, one, two, zf, za, zb, layer, gc,
):
    row_at, lane, across, along, across_end, along_end, domain = places()
    clear_edges((f, one, two, zf, za, zb, vel, g, gc))
    for index in range(TILES + 1):
        a, b, d, e = rows_of(index, from_low, from_high, TILES + 1)
        packed[index, 0:4, :] = a
        packed[index, 4:12, :] = b
        packed[index, 12:28, :] = got[index // 5, index % 5] if index < TILES else plate_window[...]
        packed[index, 28:36, :] = d
        packed[index, 36:40, :] = e

    short, span = lane < 64, lane < SPAN

    def slab_of(source, slab):
        head = packed[source * 5 + slab // 2]
        if slab % 2:
            head = turn(head, 64)
        tail = turn(packed[source * 5 + 4], 64 - 16 * slab)
        return jnp.where(short, head, jnp.where(span, tail, 0.0))

    def unpack(source):
        for row in range(4):
            at = source * 4 + row + 1
            speed = slab_of(source, row)
            layer[at] = jnp.broadcast_to(speed[16:24, SPAN - 1 : SPAN], (8, LANES))
            vel[at, TOP : TOP + WINDOW, :] = jnp.where(domain, speed, 0.0)
            one[at, TOP : TOP + WINDOW, :] = slab_of(source, 4 + row)

    loop(8, unpack, 1)
    layer[0] = layer[1]
    layer[LAYERS + 1] = layer[LAYERS]

    def replicated(ref, at, reach):
        centre, low, high, left, right = four(ref, at, reach)
        centre = jnp.where((across >= -reach) & (across < 0), high, centre)
        centre = jnp.where((across >= across_end) & (across < across_end + reach), low, centre)
        centre = jnp.where((along >= -reach) & (along < 0), right, centre)
        return jnp.where((along >= along_end) & (along < along_end + reach), left, centre)

    even_row, even_lane = parities()

    def coarse_log(at):
        total = middle(one, 2 * at + 1) + middle(one, 2 * at + 2)
        zb[at + 1, TOP : TOP + WINDOW, :] = pair_sum(total, even_row, even_lane) * 0.125
        for row in range(2):
            g[2 * at + row + 1, TOP : TOP + WINDOW, :] = jnp.exp(0.5 * replicated(one, 2 * at + row + 1, 1))

    loop(LAYERS // 2, coarse_log, 1)

    def coarse_g(at):
        gc[at + 1, TOP : TOP + WINDOW, :] = jnp.exp(0.5 * replicated(zb, at + 1, 2))

    loop(LAYERS // 2, coarse_g)
    g[0] = g[1]
    g[LAYERS + 1] = g[LAYERS]
    gc[0] = gc[1]
    gc[LAYERS // 2 + 1] = gc[LAYERS // 2]

    def coarse_factors(at):
        centre, total = around(gc, at + 1, 2)
        per = 1.0 / total
        cc[at] = jnp.where(domain, DAMPING * centre * per, 0.0)
        kc[at] = jnp.where(domain, (DAMPING / COARSE_FACTOR * 0.125) * per, 0.0)
        ginv[at] = 1.0 / centre

    loop(LAYERS // 2, coarse_factors)

    one[1, TOP : TOP + WINDOW, :] = packed[TILES]
    one[1, TOP : TOP + WINDOW, :] = replicated(one, 1, 1)
    plate, *beside = four(one, 1)
    beside = [plate + other for other in beside]

    def forcing(at):
        g_mid, *g_four = four(g, at + 1)
        v_mid, *v_four = four(vel, at + 1)
        depth = depth_at(at)
        level = layer[at + 1]
        depth_tall, twice = tall(depth), tall(2.0 * level)
        total_g = (g_four[0] + g_four[1]) + (g_four[2] + g_four[3])
        total = jnp.zeros((WINDOW, LANES), F32)
        for g_n, v_n, s_n in zip(g_four, v_four, beside):
            total = total + g_n * (depth_tall * s_n + twice) * (v_mid - v_n)
        for other in (at, at + 2):
            place = jnp.clip(other - 1, 0, LAYERS - 1)
            g_n = middle(g, other)
            total_g = total_g + g_n
            scale = tall(depth + depth_at(place)) * plate + tall(level + layer[other])
            total = total + g_n * scale * (v_mid - middle(vel, other))
        per = jnp.where(domain, DAMPING / total_g, 0.0)
        c[at] = g_mid * per
        big[at] = total_g * (1.0 / DAMPING)
        f[at + 1, TOP : TOP + WINDOW, :] = -0.5 * g_mid * total * per

    loop(LAYERS, forcing, 1)
    vcycle(f, one, two, zf, za, zb, g, c, big, cc, kc, ginv)

    own_lane = lanes_of((OWN, LANES))
    slot = own_lane // PART

    def finish(part):
        tile = jnp.zeros((OWN, LANES), F32)
        sent = []
        for row in range(4):
            at = 4 * part + row
            y = one[at + 1, TOP + HALO : TOP + HALO + OWN, :]
            x = y / g[at + 1, TOP + HALO : TOP + HALO + OWN, :]
            tile = jnp.where(slot == row, turn(x, PART * row - MARGIN), tile)
            nxt = -x / big[at, HALO : HALO + OWN, :]
            f_own[at] = nxt
            sent.append(nxt)
        inc[part] = tile
        for pair in range(2):
            both = jnp.where(own_lane < 64, turn(sent[2 * pair], -8), turn(sent[2 * pair + 1], 56))
            index = 2 * part + pair
            f_up[index] = both[8:16]
            f_down[index] = both[0:8]
            f_up[16 + part, 4 * pair : 4 * pair + 4, :] = both[4:8]
            f_down[16 + part, 4 * pair : 4 * pair + 4, :] = both[8:12]

    loop(8, finish, 1)


def second_kernel(
    g, c, big, cc, kc, ginv, vel, f_own, from_low, from_high, inc, label_window,
    send,
    f, one, two, zf, za, zb, rows, column, layers,
):
    row_at, lane, across, along, across_end, along_end, domain = places()
    clear_edges((f, one, two, zf, za, zb))
    half = lane < 64

    def unpack(part):
        for pair in range(2):
            index = 2 * part + pair
            rows[0:4, :] = from_low[16 + part, 4 * pair : 4 * pair + 4, :]
            rows[4:12, :] = from_low[index]
            rows[28:36, :] = from_high[index]
            rows[36:40, :] = from_high[16 + part, 4 * pair : 4 * pair + 4, :]
            both = rows[...]
            for row, shift in ((0, 8), (1, 72)):
                at = 4 * part + 2 * pair + row
                here = turn(both, shift)
                here = jnp.where(domain, here, 0.0)
                f[at + 1, TOP : TOP + WINDOW, :] = here
                f[at + 1, TOP + HALO : TOP + HALO + OWN, :] = f_own[at]

    rows[...] = jnp.zeros((WINDOW, LANES), F32)
    loop(8, unpack, 1)
    vcycle(f, one, two, zf, za, zb, g, c, big, cc, kc, ginv)

    def adjoint(at):
        two[at + 1, TOP : TOP + WINDOW, :] = middle(one, at + 1) / middle(g, at + 1)

    loop(LAYERS, adjoint)
    own = (row_at >= HALO) & (row_at < HALO + OWN) & (lane >= MARGIN) & (lane < MARGIN + PART)
    a_low = jnp.where(across == 0, 1.0, 0.5)
    a_high = jnp.where(across == across_end - 1, 1.0, 0.5)
    v_low = jnp.where(along == 0, 1.0, 0.5)
    v_high = jnp.where(along == along_end - 1, 1.0, 0.5)
    column[...] = jnp.zeros((WINDOW, LANES), F32)

    def density(at):
        g_mid, *g_four = four(g, at + 1)
        v_mid, *v_four = four(vel, at + 1)
        x_mid, *x_four = four(two, at + 1)
        total = jnp.zeros((WINDOW, LANES), F32)
        for h, g_n, v_n, x_n in zip((a_low, a_high, v_low, v_high), g_four, v_four, x_four):
            total = total + h * g_n * (x_n - x_mid) * (v_n - v_mid)
        for other, end in ((at, 0), (at + 2, LAYERS + 1)):
            h = jnp.where(other == end, 1.0, 0.5)
            total = total + h * middle(g, other) * (middle(two, other) - x_mid) * (middle(vel, other) - v_mid)
        total = jnp.where(own, g_mid * total, 0.0)
        column[...] += tall(depth_at(at)) * total
        folded = jnp.sum(total.reshape(WINDOW // 8, 8, LANES), axis=0)
        layers[pl.ds(at, 1), :] = jnp.sum(folded, axis=0, keepdims=True)

    loop(LAYERS, density, 1)

    labels = label_window[...]
    high, low = labels >> 7, labels & 127
    sums = column[HALO : HALO + OWN, :]
    kind = lax.broadcasted_iota(jnp.int32, (4, LANES), 0)
    place = lax.broadcasted_iota(jnp.int32, (LANES, LANES), 0)
    left, right = [], []
    for at in range(OWN):
        value = jnp.where(high[at : at + 1, :] == kind, sums[at : at + 1, :], 0.0)
        top = value.astype(jnp.bfloat16).astype(F32)
        rest = value - top
        mid = rest.astype(jnp.bfloat16).astype(F32)
        left.append(jnp.concatenate([top, mid, rest - mid, jnp.zeros_like(top)], axis=0).astype(jnp.bfloat16))
        right.append(jnp.where(low[at : at + 1, :] == place, 1.0, 0.0).astype(jnp.bfloat16))
    product = lax.dot_general(
        jnp.concatenate(left, axis=1),
        jnp.concatenate(right, axis=1),
        (((1,), (1,)), ((), ())),
        preferred_element_type=F32,
    )
    segments = (product[0:4] + product[4:8]) + product[8:12]

    slot = lanes_of((OWN, LANES)) // PART

    def pack(part):
        tile = jnp.zeros((OWN, LANES), F32)
        for row in range(4):
            x = two[4 * part + row + 1, TOP + HALO : TOP + HALO + OWN, :]
            tile = jnp.where(slot == row, turn(x, PART * row - MARGIN), tile)
        send[part, 0:16, :] = inc[part]
        send[part, 16:32, :] = tile
        send[part, 32:36, :] = segments
        send[part, 36:40, :] = layers[pl.ds(4 * part, 4), :]

    loop(8, pack, 1)


def place_kernel(got, inc, adj, spread):
    lane = lanes_of((OWN, LANES))
    slot = lane // PART
    for out, start in ((inc, 0), (adj, 16)):
        for row in range(4):
            for half in range(2):
                tile = jnp.zeros((OWN, LANES), F32)
                for source in range(4):
                    piece = got[4 * half + source, start : start + 16, :]
                    tile = jnp.where(slot == source, turn(piece, PART * (source - row)), tile)
                out[row, :, half * LANES : (half + 1) * LANES] = tile
    total = got[0, 32:40, :]
    for source in range(1, 8):
        total = total + got[source, 32:40, :]
    for other in range(64):
        spread[other] = total


def shards(velocity, log_visc, labels, seg_dir, layer_dir):
    vert = lax.axis_size("vert")
    across = lax.axis_size("au")
    ahead = [(i, (i + 1) % vert) for i in range(vert)]
    back = [((i + 1) % vert, i) for i in range(vert)]
    upward = [(i, (i + 1) % across) for i in range(across)]
    downward = [((i + 1) % across, i) for i in range(across)]

    left, right, plate = call(edge_kernel, (sds(3, OWN, LANES), sds(3, OWN, LANES), sds(OWN, 2 * LANES)))(
        velocity, log_visc, labels, seg_dir.reshape(4, LANES)
    )
    before = lax.ppermute(right, "vert", ahead)
    after = lax.ppermute(left, "vert", back)
    vmem = pl.BlockSpec(memory_space=pltpu.VMEM)
    send, plate_window, label_window = pl.pallas_call(
        window_kernel,
        out_shape=(sds(8, 5, OWN, LANES), sds(OWN, LANES), jax.ShapeDtypeStruct((OWN, LANES), jnp.int32)),
        in_specs=[vmem] * 6 + [pl.BlockSpec(memory_space=pltpu.SMEM)],
        compiler_params=pltpu.CompilerParams(vmem_limit_bytes=VMEM_LIMIT),
    )(velocity, log_visc, labels, plate, before, after, layer_dir)
    got = lax.all_to_all(send, "row", 0, 0, tiled=True)
    up, down = call(rows_kernel, (sds(62, 8, LANES), sds(62, 8, LANES)))(got, plate_window)
    from_low = lax.ppermute(up, "au", upward)
    from_high = lax.ppermute(down, "au", downward)
    fine = sds(LAYERS, WINDOW, LANES)
    fine_padded = sds(LAYERS + 2, PAD_ROWS, LANES)
    coarse = sds(LAYERS // 2, WINDOW, LANES)
    fine_scratch = pltpu.VMEM((LAYERS + 2, PAD_ROWS, LANES), F32)
    coarse_scratch = pltpu.VMEM((LAYERS // 2 + 2, PAD_ROWS, LANES), F32)
    window_scratch = pltpu.VMEM((WINDOW, LANES), F32)
    *factors, f_own, f_up, f_down, inc = call(
        first_kernel,
        (fine_padded, fine, fine, coarse, coarse, coarse, fine_padded)
        + (sds(LAYERS, OWN, LANES), sds(24, 8, LANES), sds(24, 8, LANES), sds(8, OWN, LANES)),
        [pltpu.VMEM((TILES + 1, WINDOW, LANES), F32)]
        + [fine_scratch] * 3
        + [coarse_scratch] * 3
        + [pltpu.VMEM((LAYERS + 2, 8, LANES), F32), coarse_scratch],
    )(got, plate_window, from_low, from_high)
    from_low = lax.ppermute(f_up, "au", upward)
    from_high = lax.ppermute(f_down, "au", downward)
    send = call(
        second_kernel,
        sds(8, 40, LANES),
        [fine_scratch] * 3
        + [coarse_scratch] * 3
        + [window_scratch, window_scratch, pltpu.VMEM((LAYERS, LANES), F32)],
    )(*factors, f_own, from_low, from_high, inc, label_window)
    got = lax.all_to_all(send, "row", 0, 0, tiled=True)
    field = sds(4, OWN, 8 * PART)
    increment, adjoint, spread = call(place_kernel, (field, field, sds(64, 8, LANES)))(got)
    parts = lax.all_to_all(spread, ("au", "vert"), 0, 0, tiled=True)
    total = jnp.sum(parts, axis=0)
    total_rows = LAYERS
    total_across = across * OWN
    total_along = vert * 8 * PART
    seg_scale = 1.0 / (total_rows * total_across * total_along / NSEG) ** 0.5
    layer_scale = 1.0 / (total_across * total_along) ** 0.5
    hv_segments = total[0:4].reshape(NSEG) * seg_scale
    hv_layers = jnp.sum(total[4:8], axis=1) * layer_scale
    return increment, adjoint, hv_segments, hv_layers


def solution(mesh):
    in_specs = (P("row", "au", "vert"), P("row", "au", "vert"), P("au", "vert"), P(), P("row"))
    out_specs = (P("row", "au", "vert"), P("row", "au", "vert"), P(), P("row"))
    return jax.shard_map(shards, mesh=mesh, in_specs=in_specs, out_specs=out_specs, check_vma=False)
```

```python
import jax
import jax.numpy as jnp
from jax import lax
from jax.experimental import pallas as pl
from jax.experimental.pallas import tpu as pltpu
from jax.sharding import PartitionSpec as P

NSEG = 512
DAMPING = 0.7
KEEP = 1.0 - DAMPING
COARSE_FACTOR = 0.25

LAYERS = 32
OWN = 16
HALO = 12
WINDOW = OWN + 2 * HALO
PART = 32
MARGIN = 24
SPAN = PART + 2 * MARGIN
LANES = 128
TOP = 8
HALF = WINDOW // 2
HALF_ROWS = 40
PAD_ROWS = WINDOW + 2 * TOP
TILES = 40
F32 = jnp.float32
VMEM_LIMIT = 48 * 1024 * 1024


def lanes_of(shape):
    return lax.broadcasted_iota(jnp.int32, shape, len(shape) - 1)


def turn(values, amount):
    return pltpu.roll(values, amount % LANES, values.ndim - 1)


def call(kernel, outs, scratch=(), **more):
    return pl.pallas_call(
        kernel,
        out_shape=outs,
        **more,
        scratch_shapes=list(scratch),
        compiler_params=pltpu.CompilerParams(vmem_limit_bytes=VMEM_LIMIT),
    )


def sds(*shape):
    return jax.ShapeDtypeStruct(shape, F32)


def edge_kernel(vel_in, log_in, lab_in, seg_in, left, right, plate, vel, log, lab, seg, sems):
    copies = [
        pltpu.make_async_copy(source, target, sems.at[number])
        for number, (source, target) in enumerate(((vel_in, vel), (log_in, log), (lab_in, lab), (seg_in, seg)))
    ]
    for copy in copies:
        copy.start()
    for copy in copies:
        copy.wait()
    for top in (0, 8):
        for half in range(2):
            labels = lab[top : top + 8, half * LANES : (half + 1) * LANES]
            low = labels & 127
            high = labels >> 7
            value = jnp.zeros((8, LANES), F32)
            for part in range(4):
                table = jnp.broadcast_to(seg[part : part + 1, :], (8, LANES))
                got = jnp.take_along_axis(table, low, axis=1, mode="promise_in_bounds")
                value = jnp.where(high == part, got, value)
            plate[top : top + 8, half * LANES : (half + 1) * LANES] = value
    slot = lanes_of((OWN, LANES)) // PART
    for group, field in enumerate((vel, log)):
        first = field[0, :, 0:LANES]
        last = turn(field[0, :, LANES : 2 * LANES], MARGIN)
        for row in range(1, 4):
            first = jnp.where(slot == row, turn(field[row, :, 0:LANES], PART * row), first)
            last = jnp.where(slot == row, turn(field[row, :, LANES : 2 * LANES], PART * row + MARGIN), last)
        left[group] = first
        right[group] = last
    left[2] = plate[:, 0:LANES]
    right[2] = turn(plate[:, LANES : 2 * LANES], MARGIN)


PIECES = (
    ((0, 0, 0, 80),),
    ((1, 0, 0, 80),),
    ((2, 0, 0, 80),),
    ((3, 0, 0, 80),),
    ((4, 0, 0, 80),),
    ((0, 80, 0, 48), (1, 80, 48, 32)),
    ((1, 112, 0, 16), (2, 80, 16, 48), (3, 80, 64, 16)),
    ((3, 96, 0, 32), (4, 80, 32, 48)),
)


def window_kernel(vel, log, layer, send):
    lane = lanes_of((OWN, LANES))
    turned = {}

    def at(slab, half, amount):
        key = (slab, half, amount % LANES)
        if key not in turned:
            field = (vel, log)[slab // 4]
            turned[key] = turn(field[slab % 4, :, half * LANES : (half + 1) * LANES], amount)
        return turned[key]

    for part in range(8):
        tiles = [None] * 5
        for slab, pieces in enumerate(PIECES):
            for tile, start, first, count in pieces:
                shift = start - first
                amount = MARGIN - PART * part + shift
                edge = LANES + MARGIN - PART * part + shift
                if edge >= start + count:
                    wide = at(slab, 0, amount)
                elif edge <= start:
                    wide = at(slab, 1, amount)
                else:
                    wide = jnp.where(lane < edge, at(slab, 0, amount), at(slab, 1, amount))
                if slab < 4:
                    wide = jnp.where(lane == SPAN - 1, layer[slab], wide)
                if tiles[tile] is None:
                    tiles[tile] = wide
                else:
                    tiles[tile] = jnp.where((lane >= start) & (lane < start + count), wide, tiles[tile])
        for tile in range(5):
            send[part, tile] = tiles[tile]


def patch_kernel(sent, plate, lab, left, right, from_left, from_right, send, plate_window, label_window):
    lane = lanes_of((OWN, LANES))
    place = lane % PART
    first = lax.axis_index("vert") == 0
    last = lax.axis_index("vert") == lax.axis_size("vert") - 1
    before, after = [], []
    for group in range(3):
        low, high = from_left[group], from_right[group]
        if group == 0:
            low_inner = jnp.where(place >= MARGIN - 2, 0.0, low)
            high_inner = jnp.where(place < 2, 0.0, high)
        else:
            low_inner = jnp.where(place == MARGIN - 1, turn(left[group], MARGIN - 1), low)
            low_inner = jnp.where(place == MARGIN - 2, turn(left[group], MARGIN - 3), low_inner)
            high_inner = jnp.where(place == 0, turn(right[group], 1 - MARGIN), high)
            high_inner = jnp.where(place == 1, turn(right[group], 3 - MARGIN), high_inner)
        before.append(jnp.where(first, low_inner, low))
        after.append(jnp.where(last, high_inner, high))
    for part in range(1, 7):
        send[part] = sent[part]
    for part, edges, begin, stop in ((0, before, 0, MARGIN), (7, after, SPAN - MARGIN, SPAN)):
        tiles = [sent[part, tile] for tile in range(5)]
        for slab, pieces in enumerate(PIECES):
            group, row = slab // 4, slab % 4
            end = SPAN - 1 if group == 0 and stop == SPAN else stop
            for tile, start, head, count in pieces:
                low, high = max(begin, head), min(end, head + count)
                if low >= high:
                    continue
                shift = start - head
                moved = turn(edges[group], shift + begin - PART * row)
                tiles[tile] = jnp.where((lane >= low + shift) & (lane < high + shift), moved, tiles[tile])
        for tile in range(5):
            send[part, tile] = tiles[tile]
    part = lax.axis_index("row")
    shift = PART * (part % 4)
    one, two = turn(plate[:, 0:LANES], MARGIN), turn(plate[:, LANES : 2 * LANES], MARGIN)
    head = lane < MARGIN
    tiles = (
        jnp.where(head, before[2], one),
        jnp.where(head, one, two),
        jnp.where(head, two, turn(after[2], MARGIN)),
    )
    late = part >= 4
    here = jnp.where(late, tiles[1], tiles[0])
    there = jnp.where(late, tiles[2], tiles[1])
    back = (LANES - shift) % LANES
    plate_window[...] = jnp.where(lane < LANES - shift, pltpu.roll(here, back, 1), pltpu.roll(there, back, 1))
    labels = jnp.where(late, lab[:, LANES : 2 * LANES], lab[:, 0:LANES])
    label_window[...] = pltpu.roll(labels, (LANES + MARGIN - shift) % LANES, 1)


def rows_kernel(got, plate_window, up, down):
    def tile(index):
        if index < TILES:
            return got[index // 5, index % 5]
        return plate_window[...]

    for index in range(TILES + 1):
        values = tile(index)
        at = TILES + 1 + index // 2
        half = 4 * (index % 2)
        up[index] = values[8:16]
        down[index] = values[0:8]
        up[at, half : half + 4, :] = values[4:8]
        down[at, half : half + 4, :] = values[8:12]


def rows_of(index, up, down, total):
    at = total + index // 2
    half = 4 * (index % 2)
    return up[at, half : half + 4, :], up[index], down[index], down[at, half : half + 4, :]


def places(rows=WINDOW):
    step = WINDOW // rows
    row_at = lax.broadcasted_iota(jnp.int32, (rows, LANES), 0)
    lane = lanes_of((rows, LANES))
    across = step * row_at + (lax.axis_index("au") * OWN - HALO)
    along = lane + (lax.axis_index("vert") * (8 * PART) + lax.axis_index("row") * PART - MARGIN)
    across_end = lax.axis_size("au") * OWN
    along_end = lax.axis_size("vert") * 8 * PART
    domain = (across >= 0) & (across < across_end) & (along >= 0) & (along < along_end) & (lane < SPAN)
    return row_at, lane, across, along, across_end, along_end, domain


def middle(ref, at, rows=WINDOW, top=TOP):
    return ref[at, top : top + rows, :]


def four(ref, at, rows=WINDOW, reach=1, top=TOP):
    centre = middle(ref, at, rows, top)
    return (
        centre,
        ref[at, top - 1 : top - 1 + rows, :],
        ref[at, top + 1 : top + 1 + rows, :],
        turn(centre, reach),
        turn(centre, -reach),
    )


def around(ref, at, rows=WINDOW, reach=1):
    centre, low, high, left, right = four(ref, at, rows, reach)
    total = (low + high) + (left + right)
    return centre, total + (middle(ref, at - 1, rows) + middle(ref, at + 1, rows))


def pair_sum(values, spare, even_lane):
    spare[...] = values
    total = spare[pl.ds(0, HALF, 2), :] + spare[pl.ds(1, HALF, 2), :]
    return total + jnp.where(even_lane, turn(total, -1), turn(total, 1))


def clear_edges(refs, rows=WINDOW):
    row = jnp.zeros((1, LANES), F32)
    slab = jnp.zeros((rows, LANES), F32)
    for ref in refs:
        last = ref.shape[0] - 1
        for at in range(1, last):
            ref[at, TOP - 1 : TOP, :] = row
            ref[at, TOP + rows : TOP + rows + 1, :] = row
        ref[0, TOP : TOP + rows, :] = slab
        ref[last, TOP : TOP + rows, :] = slab


def smooth(out, values, source, factor, count, rows=WINDOW, reach=1):
    for at in range(count):
        centre, total = around(values, at + 1, rows, reach)
        if source is None:
            result = (1.0 + KEEP) * centre + factor[at] * total
        else:
            result = (KEEP * centre + middle(source, at + 1, rows)) + factor[at] * total
        out[at + 1, TOP : TOP + rows, :] = result


def vcycle(f, one, two, zf, za, zb, spare, g, c, big, cc, kc, ginv):
    even_lane = lanes_of((HALF, LANES)) % 2 == 0
    coarse = (LAYERS // 2, HALF, 2)
    smooth(two, f, None, c, LAYERS)

    def leftover(at):
        centre, total = around(two, at + 1)
        return big[at] * ((middle(f, at + 1) - DAMPING * centre) + c[at] * total)

    for at in range(LAYERS // 2):
        total = leftover(2 * at) + leftover(2 * at + 1)
        zf[at + 1, TOP : TOP + HALF, :] = kc[at] * pair_sum(total, spare.at[at], even_lane)
    smooth(za, zf, None, cc, *coarse)
    smooth(zb, za, zf, cc, *coarse)
    smooth(za, zb, zf, cc, *coarse)
    for at in range(LAYERS // 2):
        value = middle(za, at + 1, HALF) * ginv[at]
        spare[at, pl.ds(0, HALF, 2), :] = value
        spare[at, pl.ds(1, HALF, 2), :] = value
        value = spare[at]
        for row in (2 * at + 1, 2 * at + 2):
            one[row, TOP : TOP + WINDOW, :] = middle(two, row) + middle(g, row) * value
    smooth(two, one, f, c, LAYERS)
    smooth(one, two, f, c, LAYERS)


def depth_at(at):
    place = jnp.full((8, LANES), at, jnp.int32)
    return jnp.exp(-(LAYERS - 1 - place).astype(F32) / (LAYERS / 4.0))


def tall(values, rows=WINDOW):
    return jnp.concatenate([values] * (rows // 8), axis=0)


def first_kernel(
    got, plate_window, from_low, from_high,
    g, c, big, cc, kc, ginv, vel, x_own, f_own, f_up, f_down,
    packed, f, one, two, zf, za, zb, spare, layer, gc,
):
    domain = places()[-1]
    coarse_domain = places(HALF)[-1]
    clear_edges((f, one, two, vel, g))
    clear_edges((zf, za, zb, gc), HALF)
    for index in range(TILES + 1):
        a, b, d, e = rows_of(index, from_low, from_high, TILES + 1)
        packed[index, 0:4, :] = a
        packed[index, 4:12, :] = b
        packed[index, 12:28, :] = got[index // 5, index % 5] if index < TILES else plate_window[...]
        packed[index, 28:36, :] = d
        packed[index, 36:40, :] = e

    def mirror(pairs):
        speed = lanes_of((1, LANES)) < SPAN
        for index in range(TILES + 1):
            for target, source in pairs:
                value = packed[index, source : source + 1, :]
                if index < TILES and index % 5 < 4:
                    value = jnp.where(speed, 0.0, value)
                packed[index, target : target + 1, :] = value

    @pl.when(lax.axis_index("au") == 0)
    def _():
        mirror(((HALO - 1, HALO), (HALO - 2, HALO + 1)))

    @pl.when(lax.axis_index("au") == lax.axis_size("au") - 1)
    def _():
        mirror(((HALO + OWN, HALO + OWN - 1), (HALO + OWN + 1, HALO + OWN - 2)))

    lane = lanes_of((WINDOW, LANES))
    even_lane = lanes_of((HALF, LANES)) % 2 == 0

    def slab_of(source, slab):
        result = jnp.zeros((WINDOW, LANES), F32)
        for tile, start, first, count in reversed(PIECES[slab]):
            result = jnp.where(lane < first + count, turn(packed[source * 5 + tile], first - start), result)
        return result

    for source in range(8):
        logs = []
        for row in range(4):
            at = source * 4 + row + 1
            speed = slab_of(source, row)
            layer[at] = jnp.broadcast_to(speed[16:24, SPAN - 1 : SPAN], (8, LANES))
            vel[at, TOP : TOP + WINDOW, :] = speed
            logs.append(slab_of(source, 4 + row))
            g[at, TOP : TOP + WINDOW, :] = jnp.exp(0.5 * logs[-1])
        for pair in range(2):
            at = 2 * source + pair
            total = pair_sum(logs[2 * pair] + logs[2 * pair + 1], spare.at[at], even_lane)
            gc[at + 1, TOP : TOP + HALF, :] = jnp.exp(0.0625 * total)
    layer[0] = layer[1]
    layer[LAYERS + 1] = layer[LAYERS]
    g[0] = g[1]
    g[LAYERS + 1] = g[LAYERS]
    gc[0] = gc[1]
    gc[LAYERS // 2 + 1] = gc[LAYERS // 2]

    for at in range(LAYERS // 2):
        centre, total = around(gc, at + 1, HALF, 2)
        per = jnp.where(coarse_domain, DAMPING / total, 0.0)
        cc[at] = centre * per
        kc[at] = (0.125 / COARSE_FACTOR) * per
        ginv[at] = 1.0 / centre

    plate = packed[TILES]
    one[1, TOP : TOP + WINDOW, :] = plate
    beside = [plate + other for other in four(one, 1)[1:]]
    across_layers = None
    for at in range(LAYERS):
        g_mid, *g_four = four(g, at + 1)
        v_mid, *v_four = four(vel, at + 1)
        depth = depth_at(at)
        level = layer[at + 1]
        depth_tall, twice = tall(depth), tall(2.0 * level)
        total_g = (g_four[0] + g_four[1]) + (g_four[2] + g_four[3])
        total_g = total_g + (middle(g, at) + middle(g, at + 2))
        total = jnp.zeros((WINDOW, LANES), F32)
        for g_n, v_n, s_n in zip(g_four, v_four, beside):
            total = total + g_n * (depth_tall * s_n + twice) * (v_mid - v_n)
        total = g_mid * total
        for other in (at, at + 2):
            place = min(max(other - 1, 0), LAYERS - 1)
            if other == at and at > 0:
                total = total - across_layers
                continue
            scale = tall(depth + depth_at(place)) * plate + tall(level + layer[other])
            across_layers = (g_mid * middle(g, other)) * scale * (v_mid - middle(vel, other))
            total = total + across_layers
        per = jnp.where(domain, DAMPING / total_g, 0.0)
        c[at] = g_mid * per
        big[at] = total_g * (1.0 / DAMPING)
        f[at + 1, TOP : TOP + WINDOW, :] = -0.5 * total * per
    vcycle(f, one, two, zf, za, zb, spare, g, c, big, cc, kc, ginv)

    own_lane = lanes_of((OWN, LANES))
    sent = []
    for at in range(LAYERS):
        ratio = 1.0 / g[at + 1, TOP + HALO : TOP + HALO + OWN, :]
        x = one[at + 1, TOP + HALO : TOP + HALO + OWN, :] * ratio
        x_own[at] = x
        nxt = -(x * (c[at, HALO : HALO + OWN, :] * ratio))
        f_own[at] = nxt
        sent.append(nxt)
    for index in range(16):
        both = jnp.where(own_lane < 64, turn(sent[2 * index], -8), turn(sent[2 * index + 1], 56))
        start = 4 * (index % 2)
        f_up[index] = both[8:16]
        f_down[index] = both[0:8]
        f_up[16 + index // 2, start : start + 4, :] = both[4:8]
        f_down[16 + index // 2, start : start + 4, :] = both[8:12]


def side_kernel(x_own, label_window, inc, ones):
    slot = lanes_of((OWN, LANES)) // PART
    for part in range(8):
        tile = turn(x_own[4 * part], -MARGIN)
        for row in range(1, 4):
            tile = jnp.where(slot == row, turn(x_own[4 * part + row], PART * row - MARGIN), tile)
        inc[part] = tile
    low = label_window[...] & 127
    place = lax.broadcasted_iota(jnp.int32, (LANES, LANES), 0)
    for at in range(OWN):
        hit = jnp.where(low[at : at + 1, :] == place, 1.0, 0.0)
        ones[:, at * LANES : (at + 1) * LANES] = hit.astype(jnp.bfloat16)


INNER = 24
SKIP = 8


def second_kernel(
    g, c, big, cc, kc, ginv, vel, f_own, from_low, from_high, inc, label_window, ones,
    send,
    f, one, two, zf, za, zb, spare, layers,
):
    _, lane, _, _, _, _, domain = places()
    clear_edges((f, one, two))
    clear_edges((zf, za, zb), HALF)
    for index in range(16):
        start = 4 * (index % 2)
        spare[index, 0:4, :] = from_low[16 + index // 2, start : start + 4, :]
        spare[index, 4:12, :] = from_low[index]
        spare[index, 28:36, :] = from_high[index]
        spare[index, 36:40, :] = from_high[16 + index // 2, start : start + 4, :]
        for row, shift in ((0, 8), (1, 72)):
            at = 2 * index + row
            if row == 0:
                spare[index, HALO : HALO + OWN, :] = turn(f_own[at], -8)
            else:
                spare[index, HALO : HALO + OWN, :] = turn(f_own[at], 56)
            f[at + 1, TOP : TOP + WINDOW, :] = jnp.where(domain, turn(spare[index], shift), 0.0)
    vcycle(f, one, two, zf, za, zb, spare, g, c, big, cc, kc, ginv)

    top = TOP + SKIP
    for at in range(LAYERS):
        two[at + 1, top : top + INNER, :] = middle(one, at + 1, INNER, top) / middle(g, at + 1, INNER, top)
    row_at = SKIP + lax.broadcasted_iota(jnp.int32, (INNER, LANES), 0)
    lane = lanes_of((INNER, LANES))
    across = row_at + (lax.axis_index("au") * OWN - HALO)
    along = lane + (lax.axis_index("vert") * (8 * PART) + lax.axis_index("row") * PART - MARGIN)
    own = (row_at >= HALO) & (row_at < HALO + OWN) & (lane >= MARGIN) & (lane < MARGIN + PART)
    shares = [
        jnp.where(edge, 1.0, 0.5)
        for edge in (
            across == 0,
            across == lax.axis_size("au") * OWN - 1,
            along == 0,
            along == lax.axis_size("vert") * 8 * PART - 1,
        )
    ]
    column = jnp.zeros((INNER, LANES), F32)
    for at in range(LAYERS):
        g_mid, *g_four = four(g, at + 1, INNER, 1, top)
        v_mid, *v_four = four(vel, at + 1, INNER, 1, top)
        x_mid, *x_four = four(two, at + 1, INNER, 1, top)
        total = jnp.zeros((INNER, LANES), F32)
        for share, g_n, v_n, x_n in zip(shares, g_four, v_four, x_four):
            total = total + (share * g_n) * ((x_n - x_mid) * (v_n - v_mid))
        for other, end in ((at, 0), (at + 2, LAYERS + 1)):
            share = 1.0 if other == end else 0.5
            x_n, v_n = middle(two, other, INNER, top), middle(vel, other, INNER, top)
            total = total + (share * middle(g, other, INNER, top)) * ((x_n - x_mid) * (v_n - v_mid))
        total = jnp.where(own, g_mid * total, 0.0)
        column = column + tall(depth_at(at), INNER) * total
        folded = jnp.sum(total.reshape(INNER // 8, 8, LANES), axis=0)
        layers[at : at + 1, :] = jnp.sum(folded, axis=0, keepdims=True)

    high = label_window[...] >> 7
    sums = column[HALO - SKIP : HALO - SKIP + OWN, :]
    kind = lax.broadcasted_iota(jnp.int32, (4, LANES), 0)
    left = []
    for at in range(OWN):
        value = jnp.where(high[at : at + 1, :] == kind, sums[at : at + 1, :], 0.0)
        first = value.astype(jnp.bfloat16).astype(F32)
        rest = value - first
        then = rest.astype(jnp.bfloat16).astype(F32)
        left.append(jnp.concatenate([first, then, rest - then, jnp.zeros_like(first)], axis=0).astype(jnp.bfloat16))
    product = lax.dot_general(
        jnp.concatenate(left, axis=1), ones[...], (((1,), (1,)), ((), ())), preferred_element_type=F32
    )
    segments = (product[0:4] + product[4:8]) + product[8:12]

    slot = lanes_of((OWN, LANES)) // PART
    for part in range(8):
        tile = turn(two[4 * part + 1, TOP + HALO : TOP + HALO + OWN, :], -MARGIN)
        for row in range(1, 4):
            x = two[4 * part + row + 1, TOP + HALO : TOP + HALO + OWN, :]
            tile = jnp.where(slot == row, turn(x, PART * row - MARGIN), tile)
        send[part, 0:16, :] = inc[part]
        send[part, 16:32, :] = tile
        send[part, 32:36, :] = segments
        send[part, 36:40, :] = layers[4 * part : 4 * part + 4, :]


def place_kernel(got, inc, adj, spread):
    lane = lanes_of((OWN, LANES))
    slot = lane // PART
    for out, start in ((inc, 0), (adj, 16)):
        for row in range(4):
            for half in range(2):
                tile = jnp.zeros((OWN, LANES), F32)
                for source in range(4):
                    piece = got[4 * half + source, start : start + 16, :]
                    tile = jnp.where(slot == source, turn(piece, PART * (source - row)), tile)
                out[row, :, half * LANES : (half + 1) * LANES] = tile
    total = got[0, 32:40, :]
    for source in range(1, 8):
        total = total + got[source, 32:40, :]
    level = jnp.zeros((1, LANES), F32)
    lane = lanes_of((1, LANES))
    for row in range(4):
        level = jnp.where(lane == row, jnp.sum(total[4 + row : 5 + row, :], axis=1, keepdims=True), level)
    pieces = [total[row : row + 1, :] for row in range(4)] + [level]
    line = jnp.concatenate(pieces, axis=1)
    for other in range(spread.shape[0]):
        spread[other] = line


def total_kernel(parts, segments, layers):
    cells = LAYERS * lax.axis_size("au") * OWN * lax.axis_size("vert") * 8 * PART
    total = jnp.sum(parts[...], axis=0)
    for row in range(4):
        segments[row : row + 1, :] = total[:, row * LANES : (row + 1) * LANES] * (1.0 / (cells / NSEG) ** 0.5)
    layers[...] = total[:, 4 * LANES : 4 * LANES + 4] * (1.0 / (cells / LAYERS) ** 0.5)


def shards(velocity, log_visc, labels, seg_dir, layer_dir):
    vert = lax.axis_size("vert")
    across = lax.axis_size("au")
    ahead = [(i, (i + 1) % vert) for i in range(vert)]
    back = [((i + 1) % vert, i) for i in range(vert)]
    upward = [(i, i + 1) for i in range(across - 1)]
    downward = [(i + 1, i) for i in range(across - 1)]
    vmem = pl.BlockSpec(memory_space=pltpu.VMEM)
    hbm = pl.BlockSpec(memory_space=pltpu.HBM)
    labels_like = jax.ShapeDtypeStruct((OWN, 2 * LANES), jnp.int32)
    label_tile = jax.ShapeDtypeStruct((OWN, LANES), jnp.int32)
    edges, field = sds(3, OWN, LANES), sds(4, OWN, 2 * LANES)

    left, right, plate, vel, log, lab = call(
        edge_kernel,
        (edges, edges, sds(OWN, 2 * LANES), field, field, labels_like),
        [pltpu.VMEM((4, LANES), F32), pltpu.SemaphoreType.DMA((4,))],
        in_specs=[hbm] * 4,
    )(velocity, log_visc, labels, seg_dir.reshape(4, LANES))
    from_left = lax.ppermute(right, "vert", ahead)
    from_right = lax.ppermute(left, "vert", back)
    send = call(
        window_kernel,
        sds(8, 5, OWN, LANES),
        in_specs=[vmem, vmem, pl.BlockSpec(memory_space=pltpu.SMEM)],
    )(vel, log, layer_dir)
    send, plate_window, label_window = call(
        patch_kernel, (sds(8, 5, OWN, LANES), sds(OWN, LANES), label_tile)
    )(send, plate, lab, left, right, from_left, from_right)
    got = lax.all_to_all(send, "row", 0, 0, tiled=True)
    up, down = call(rows_kernel, (sds(62, 8, LANES), sds(62, 8, LANES)))(got, plate_window)
    from_low = lax.ppermute(up, "au", upward)
    from_high = lax.ppermute(down, "au", downward)
    fine = sds(LAYERS, WINDOW, LANES)
    fine_padded = sds(LAYERS + 2, PAD_ROWS, LANES)
    coarse = sds(LAYERS // 2, HALF, LANES)
    own = sds(LAYERS, OWN, LANES)
    fine_scratch = pltpu.VMEM((LAYERS + 2, PAD_ROWS, LANES), F32)
    coarse_scratch = pltpu.VMEM((LAYERS // 2 + 2, HALF_ROWS, LANES), F32)
    spare = pltpu.VMEM((LAYERS // 2, WINDOW, LANES), F32)
    *factors, x_own, f_own, f_up, f_down = call(
        first_kernel,
        (fine_padded, fine, fine, coarse, coarse, coarse, fine_padded)
        + (own, own, sds(24, 8, LANES), sds(24, 8, LANES)),
        [pltpu.VMEM((TILES + 1, WINDOW, LANES), F32)]
        + [fine_scratch] * 3
        + [coarse_scratch] * 3
        + [spare, pltpu.VMEM((LAYERS + 2, 8, LANES), F32), coarse_scratch],
    )(got, plate_window, from_low, from_high)
    from_low = lax.ppermute(f_up, "au", upward)
    from_high = lax.ppermute(f_down, "au", downward)
    inc, ones = call(
        side_kernel, (sds(8, OWN, LANES), jax.ShapeDtypeStruct((LANES, OWN * LANES), jnp.bfloat16))
    )(x_own, label_window)
    send = call(
        second_kernel,
        sds(8, 40, LANES),
        [fine_scratch] * 3 + [coarse_scratch] * 3 + [spare, pltpu.VMEM((LAYERS, LANES), F32)],
    )(*factors, f_own, from_low, from_high, inc, label_window, ones)
    got = lax.all_to_all(send, "row", 0, 0, tiled=True)
    increment, adjoint, spread = call(place_kernel, (field, field, sds(across * vert, 1, 5 * LANES)))(got)
    parts = lax.all_to_all(spread, ("au", "vert"), 0, 0, tiled=True)
    hv_segments, hv_layers = call(total_kernel, (sds(4, LANES), sds(1, 4)))(parts)
    return increment, adjoint, hv_segments.reshape(NSEG), hv_layers.reshape(4)


def solution(mesh):
    in_specs = (P("row", "au", "vert"), P("row", "au", "vert"), P("au", "vert"), P(), P("row"))
    out_specs = (P("row", "au", "vert"), P("row", "au", "vert"), P(), P("row"))
    return jax.shard_map(shards, mesh=mesh, in_specs=in_specs, out_specs=out_specs, check_vma=False)
```

```python
import jax
import jax.numpy as jnp
from jax import lax
from jax.experimental import pallas as pl
from jax.experimental.pallas import tpu as pltpu
from jax.sharding import PartitionSpec as P

NSEG = 512
DAMPING = 0.7
KEEP = 1.0 - DAMPING
COARSE_FACTOR = 0.25

LAYERS = 32
OWN = 16
HALO = 12
WINDOW = OWN + 2 * HALO
PART = 32
MARGIN = 24
SPAN = PART + 2 * MARGIN
LANES = 128
TOP = 8
HALF = WINDOW // 2
HALF_ROWS = 40
PAD_ROWS = WINDOW + 2 * TOP
TILES = 40
F32 = jnp.float32
VMEM_LIMIT = 48 * 1024 * 1024
EDGE_LIMIT = 56290000


def lanes_of(shape):
    return lax.broadcasted_iota(jnp.int32, shape, len(shape) - 1)


def turn(values, amount):
    return pltpu.roll(values, amount % LANES, values.ndim - 1)


def call(kernel, outs, scratch=(), limit=VMEM_LIMIT, **more):
    return pl.pallas_call(
        kernel,
        out_shape=outs,
        **more,
        scratch_shapes=list(scratch),
        compiler_params=pltpu.CompilerParams(vmem_limit_bytes=limit),
    )


def sds(*shape):
    return jax.ShapeDtypeStruct(shape, F32)


def edge_kernel(vel_in, log_in, lab_in, seg_in, left, right, plate, vel, log, lab, seg, sems):
    copies = [
        pltpu.make_async_copy(source, target, sems.at[number])
        for number, (source, target) in enumerate(((vel_in, vel), (log_in, log), (lab_in, lab), (seg_in, seg)))
    ]
    for copy in copies:
        copy.start()
    for copy in copies:
        copy.wait()
    for top in (0, 8):
        for half in range(2):
            labels = lab[top : top + 8, half * LANES : (half + 1) * LANES]
            low = labels & 127
            high = labels >> 7
            value = jnp.zeros((8, LANES), F32)
            for part in range(4):
                table = jnp.broadcast_to(seg[part : part + 1, :], (8, LANES))
                got = jnp.take_along_axis(table, low, axis=1, mode="promise_in_bounds")
                value = jnp.where(high == part, got, value)
            plate[top : top + 8, half * LANES : (half + 1) * LANES] = value
    slot = lanes_of((OWN, LANES)) // PART
    for group, field in enumerate((vel, log)):
        first = field[0, :, 0:LANES]
        last = turn(field[0, :, LANES : 2 * LANES], MARGIN)
        for row in range(1, 4):
            first = jnp.where(slot == row, turn(field[row, :, 0:LANES], PART * row), first)
            last = jnp.where(slot == row, turn(field[row, :, LANES : 2 * LANES], PART * row + MARGIN), last)
        left[group] = first
        right[group] = last
    left[2] = plate[:, 0:LANES]
    right[2] = turn(plate[:, LANES : 2 * LANES], MARGIN)


PIECES = (
    ((0, 0, 0, 80),),
    ((1, 0, 0, 80),),
    ((2, 0, 0, 80),),
    ((3, 0, 0, 80),),
    ((4, 0, 0, 80),),
    ((0, 80, 0, 48), (1, 80, 48, 32)),
    ((1, 112, 0, 16), (2, 80, 16, 48), (3, 80, 64, 16)),
    ((3, 96, 0, 32), (4, 80, 32, 48)),
)


def window_kernel(vel, log, layer, send):
    lane = lanes_of((OWN, LANES))
    turned = {}

    def at(slab, half, amount):
        key = (slab, half, amount % LANES)
        if key not in turned:
            field = (vel, log)[slab // 4]
            turned[key] = turn(field[slab % 4, :, half * LANES : (half + 1) * LANES], amount)
        return turned[key]

    for part in range(8):
        tiles = [None] * 5
        for slab, pieces in enumerate(PIECES):
            for tile, start, first, count in pieces:
                shift = start - first
                amount = MARGIN - PART * part + shift
                edge = LANES + MARGIN - PART * part + shift
                if edge >= start + count:
                    wide = at(slab, 0, amount)
                elif edge <= start:
                    wide = at(slab, 1, amount)
                else:
                    wide = jnp.where(lane < edge, at(slab, 0, amount), at(slab, 1, amount))
                if slab < 4:
                    wide = jnp.where(lane == SPAN - 1, layer[slab], wide)
                if tiles[tile] is None:
                    tiles[tile] = wide
                else:
                    tiles[tile] = jnp.where((lane >= start) & (lane < start + count), wide, tiles[tile])
        for tile in range(5):
            send[part, tile] = tiles[tile]


def patch_kernel(sent, plate, lab, left, right, from_left, from_right, send, plate_window, label_window):
    lane = lanes_of((OWN, LANES))
    place = lane % PART
    first = lax.axis_index("vert") == 0
    last = lax.axis_index("vert") == lax.axis_size("vert") - 1
    before, after = [], []
    for group in range(3):
        low, high = from_left[group], from_right[group]
        if group == 0:
            low_inner = jnp.where(place >= MARGIN - 2, 0.0, low)
            high_inner = jnp.where(place < 2, 0.0, high)
        else:
            low_inner = jnp.where(place == MARGIN - 1, turn(left[group], MARGIN - 1), low)
            low_inner = jnp.where(place == MARGIN - 2, turn(left[group], MARGIN - 3), low_inner)
            high_inner = jnp.where(place == 0, turn(right[group], 1 - MARGIN), high)
            high_inner = jnp.where(place == 1, turn(right[group], 3 - MARGIN), high_inner)
        before.append(jnp.where(first, low_inner, low))
        after.append(jnp.where(last, high_inner, high))
    for part in range(1, 7):
        send[part] = sent[part]
    for part, edges, begin, stop in ((0, before, 0, MARGIN), (7, after, SPAN - MARGIN, SPAN)):
        tiles = [sent[part, tile] for tile in range(5)]
        for slab, pieces in enumerate(PIECES):
            group, row = slab // 4, slab % 4
            end = SPAN - 1 if group == 0 and stop == SPAN else stop
            for tile, start, head, count in pieces:
                low, high = max(begin, head), min(end, head + count)
                if low >= high:
                    continue
                shift = start - head
                moved = turn(edges[group], shift + begin - PART * row)
                tiles[tile] = jnp.where((lane >= low + shift) & (lane < high + shift), moved, tiles[tile])
        for tile in range(5):
            send[part, tile] = tiles[tile]
    part = lax.axis_index("row")
    shift = PART * (part % 4)
    one, two = turn(plate[:, 0:LANES], MARGIN), turn(plate[:, LANES : 2 * LANES], MARGIN)
    head = lane < MARGIN
    tiles = (
        jnp.where(head, before[2], one),
        jnp.where(head, one, two),
        jnp.where(head, two, turn(after[2], MARGIN)),
    )
    late = part >= 4
    here = jnp.where(late, tiles[1], tiles[0])
    there = jnp.where(late, tiles[2], tiles[1])
    back = (LANES - shift) % LANES
    plate_window[...] = jnp.where(lane < LANES - shift, pltpu.roll(here, back, 1), pltpu.roll(there, back, 1))
    labels = jnp.where(late, lab[:, LANES : 2 * LANES], lab[:, 0:LANES])
    label_window[...] = pltpu.roll(labels, (LANES + MARGIN - shift) % LANES, 1)


def rows_kernel(got, plate_window, up, down):
    def tile(index):
        if index < TILES:
            return got[index // 5, index % 5]
        return plate_window[...]

    for index in range(TILES + 1):
        values = tile(index)
        at = TILES + 1 + index // 2
        half = 4 * (index % 2)
        up[index] = values[8:16]
        down[index] = values[0:8]
        up[at, half : half + 4, :] = values[4:8]
        down[at, half : half + 4, :] = values[8:12]


def rows_of(index, up, down, total):
    at = total + index // 2
    half = 4 * (index % 2)
    return up[at, half : half + 4, :], up[index], down[index], down[at, half : half + 4, :]


def places(rows=WINDOW):
    step = WINDOW // rows
    row_at = lax.broadcasted_iota(jnp.int32, (rows, LANES), 0)
    lane = lanes_of((rows, LANES))
    across = step * row_at + (lax.axis_index("au") * OWN - HALO)
    along = lane + (lax.axis_index("vert") * (8 * PART) + lax.axis_index("row") * PART - MARGIN)
    across_end = lax.axis_size("au") * OWN
    along_end = lax.axis_size("vert") * 8 * PART
    domain = (across >= 0) & (across < across_end) & (along >= 0) & (along < along_end) & (lane < SPAN)
    return row_at, lane, across, along, across_end, along_end, domain


def middle(ref, at, rows=WINDOW, top=TOP):
    return ref[at, top : top + rows, :]


def four(ref, at, rows=WINDOW, reach=1, top=TOP):
    centre = middle(ref, at, rows, top)
    return (
        centre,
        ref[at, top - 1 : top - 1 + rows, :],
        ref[at, top + 1 : top + 1 + rows, :],
        turn(centre, reach),
        turn(centre, -reach),
    )


def around(ref, at, rows=WINDOW, reach=1):
    centre, low, high, left, right = four(ref, at, rows, reach)
    total = (low + high) + (left + right)
    return centre, total + (middle(ref, at - 1, rows) + middle(ref, at + 1, rows))


def pair_sum(spare, even_lane):
    total = spare[pl.ds(0, HALF, 2), :] + spare[pl.ds(1, HALF, 2), :]
    return total + jnp.where(even_lane, turn(total, -1), turn(total, 1))


def clear_edges(refs, rows=WINDOW):
    row = jnp.zeros((1, LANES), F32)
    slab = jnp.zeros((rows, LANES), F32)
    for ref in refs:
        last = ref.shape[0] - 1
        for at in range(1, last):
            ref[at, TOP - 1 : TOP, :] = row
            ref[at, TOP + rows : TOP + rows + 1, :] = row
        ref[0, TOP : TOP + rows, :] = slab
        ref[last, TOP : TOP + rows, :] = slab


def smooth(out, values, source, factor, count, rows=WINDOW, reach=1):
    for at in range(count):
        centre, total = around(values, at + 1, rows, reach)
        if source is None:
            result = (1.0 + KEEP) * centre + factor[at] * total
        else:
            result = (KEEP * centre + middle(source, at + 1, rows)) + factor[at] * total
        out[at + 1, TOP : TOP + rows, :] = result


def vcycle(f, one, two, zf, za, zb, spare, g, c, big, cc, kc, ginv):
    even_lane = lanes_of((HALF, LANES)) % 2 == 0
    coarse = (LAYERS // 2, HALF, 2)
    smooth(two, f, None, c, LAYERS)

    def leftover(at):
        centre, total = around(two, at + 1)
        return big[at] * ((middle(f, at + 1) - DAMPING * centre) + c[at] * total)

    for at in range(LAYERS // 2):
        spare[at] = leftover(2 * at) + leftover(2 * at + 1)
    for at in range(LAYERS // 2):
        zf[at + 1, TOP : TOP + HALF, :] = kc[at] * pair_sum(spare.at[at], even_lane)
    smooth(za, zf, None, cc, *coarse)
    smooth(zb, za, zf, cc, *coarse)
    smooth(za, zb, zf, cc, *coarse)
    for at in range(LAYERS // 2):
        value = middle(za, at + 1, HALF) * ginv[at]
        spare[at, pl.ds(0, HALF, 2), :] = value
        spare[at, pl.ds(1, HALF, 2), :] = value
    for at in range(LAYERS // 2):
        value = spare[at]
        for row in (2 * at + 1, 2 * at + 2):
            one[row, TOP : TOP + WINDOW, :] = middle(two, row) + middle(g, row) * value
    smooth(two, one, f, c, LAYERS)
    smooth(one, two, f, c, LAYERS)


def depth_at(at):
    place = jnp.full((8, LANES), at, jnp.int32)
    return jnp.exp(-(LAYERS - 1 - place).astype(F32) / (LAYERS / 4.0))


def tall(values, rows=WINDOW):
    return jnp.concatenate([values] * (rows // 8), axis=0)


def first_kernel(
    got, plate_window, from_low, from_high,
    g, c, big, cc, kc, ginv, vel, x_own, f_own, f_up, f_down,
    packed, f, one, two, zf, za, zb, spare, layer, gc,
):
    domain = places()[-1]
    coarse_domain = places(HALF)[-1]
    clear_edges((f, one, two, vel, g))
    clear_edges((zf, za, zb, gc), HALF)
    for index in range(TILES + 1):
        a, b, d, e = rows_of(index, from_low, from_high, TILES + 1)
        packed[index, 0:4, :] = a
        packed[index, 4:12, :] = b
        packed[index, 12:28, :] = got[index // 5, index % 5] if index < TILES else plate_window[...]
        packed[index, 28:36, :] = d
        packed[index, 36:40, :] = e

    def mirror(pairs):
        speed = lanes_of((1, LANES)) < SPAN
        for index in range(TILES + 1):
            for target, source in pairs:
                value = packed[index, source : source + 1, :]
                if index < TILES and index % 5 < 4:
                    value = jnp.where(speed, 0.0, value)
                packed[index, target : target + 1, :] = value

    @pl.when(lax.axis_index("au") == 0)
    def _():
        mirror(((HALO - 1, HALO), (HALO - 2, HALO + 1)))

    @pl.when(lax.axis_index("au") == lax.axis_size("au") - 1)
    def _():
        mirror(((HALO + OWN, HALO + OWN - 1), (HALO + OWN + 1, HALO + OWN - 2)))

    lane = lanes_of((WINDOW, LANES))
    even_lane = lanes_of((HALF, LANES)) % 2 == 0

    def slab_of(source, slab):
        result = jnp.zeros((WINDOW, LANES), F32)
        for tile, start, first, count in reversed(PIECES[slab]):
            result = jnp.where(lane < first + count, turn(packed[source * 5 + tile], first - start), result)
        return result

    for source in range(8):
        logs = []
        for row in range(4):
            at = source * 4 + row + 1
            speed = slab_of(source, row)
            layer[at] = jnp.broadcast_to(speed[16:24, SPAN - 1 : SPAN], (8, LANES))
            vel[at, TOP : TOP + WINDOW, :] = speed
            logs.append(slab_of(source, 4 + row))
            g[at, TOP : TOP + WINDOW, :] = jnp.exp(0.5 * logs[-1])
        for pair in range(2):
            spare[2 * source + pair] = logs[2 * pair] + logs[2 * pair + 1]
    for at in range(LAYERS // 2):
        gc[at + 1, TOP : TOP + HALF, :] = jnp.exp(0.0625 * pair_sum(spare.at[at], even_lane))
    layer[0] = layer[1]
    layer[LAYERS + 1] = layer[LAYERS]
    g[0] = g[1]
    g[LAYERS + 1] = g[LAYERS]
    gc[0] = gc[1]
    gc[LAYERS // 2 + 1] = gc[LAYERS // 2]

    for at in range(LAYERS // 2):
        centre, total = around(gc, at + 1, HALF, 2)
        per = jnp.where(coarse_domain, DAMPING / total, 0.0)
        cc[at] = centre * per
        kc[at] = (0.125 / COARSE_FACTOR) * per
        ginv[at] = 1.0 / centre

    plate = packed[TILES]
    one[1, TOP : TOP + WINDOW, :] = plate
    beside = [plate + other for other in four(one, 1)[1:]]
    across_layers = None
    for at in range(LAYERS):
        g_mid, *g_four = four(g, at + 1)
        v_mid, *v_four = four(vel, at + 1)
        depth = depth_at(at)
        level = layer[at + 1]
        depth_tall, twice = tall(depth), tall(2.0 * level)
        total_g = (g_four[0] + g_four[1]) + (g_four[2] + g_four[3])
        total_g = total_g + (middle(g, at) + middle(g, at + 2))
        total = jnp.zeros((WINDOW, LANES), F32)
        for g_n, v_n, s_n in zip(g_four, v_four, beside):
            total = total + g_n * (depth_tall * s_n + twice) * (v_mid - v_n)
        total = g_mid * total
        for other in (at, at + 2):
            place = min(max(other - 1, 0), LAYERS - 1)
            if other == at and at > 0:
                total = total - across_layers
                continue
            scale = tall(depth + depth_at(place)) * plate + tall(level + layer[other])
            across_layers = (g_mid * middle(g, other)) * scale * (v_mid - middle(vel, other))
            total = total + across_layers
        per = jnp.where(domain, DAMPING / total_g, 0.0)
        c[at] = g_mid * per
        big[at] = total_g * (1.0 / DAMPING)
        f[at + 1, TOP : TOP + WINDOW, :] = -0.5 * total * per
    vcycle(f, one, two, zf, za, zb, spare, g, c, big, cc, kc, ginv)

    own_lane = lanes_of((OWN, LANES))
    sent = []
    for at in range(LAYERS):
        ratio = 1.0 / g[at + 1, TOP + HALO : TOP + HALO + OWN, :]
        x = one[at + 1, TOP + HALO : TOP + HALO + OWN, :] * ratio
        x_own[at] = x
        sent.append(-(x * (c[at, HALO : HALO + OWN, :] * ratio)))
    for index in range(16):
        both = jnp.where(own_lane < 64, turn(sent[2 * index], -8), turn(sent[2 * index + 1], 56))
        start = 4 * (index % 2)
        f_own[index] = both
        f_up[index] = both[8:16]
        f_down[index] = both[0:8]
        f_up[16 + index // 2, start : start + 4, :] = both[4:8]
        f_down[16 + index // 2, start : start + 4, :] = both[8:12]


def side_kernel(x_own, label_window, inc, ones):
    slot = lanes_of((OWN, LANES)) // PART
    for part in range(8):
        tile = turn(x_own[4 * part], -MARGIN)
        for row in range(1, 4):
            tile = jnp.where(slot == row, turn(x_own[4 * part + row], PART * row - MARGIN), tile)
        inc[part] = tile
    low = label_window[...] & 127
    place = lax.broadcasted_iota(jnp.int32, (LANES, LANES), 0)
    for at in range(OWN):
        hit = jnp.where(low[at : at + 1, :] == place, 1.0, 0.0)
        ones[:, at * LANES : (at + 1) * LANES] = hit.astype(jnp.bfloat16)


INNER = 24
SKIP = 8


def second_kernel(
    g, c, big, cc, kc, ginv, vel, f_own, from_low, from_high, inc, label_window, ones,
    send,
    f, one, two, zf, za, zb, spare, layers,
):
    _, lane, _, _, _, _, domain = places()
    clear_edges((f, one, two))
    clear_edges((zf, za, zb), HALF)
    for index in range(16):
        start = 4 * (index % 2)
        spare[index, 0:4, :] = from_low[16 + index // 2, start : start + 4, :]
        spare[index, 4:12, :] = from_low[index]
        spare[index, 28:36, :] = from_high[index]
        spare[index, 36:40, :] = from_high[16 + index // 2, start : start + 4, :]
        spare[index, HALO : HALO + OWN, :] = f_own[index]
    for index in range(16):
        both = spare[index]
        for row, shift in ((0, 8), (1, 72)):
            f[2 * index + row + 1, TOP : TOP + WINDOW, :] = jnp.where(domain, turn(both, shift), 0.0)
    vcycle(f, one, two, zf, za, zb, spare, g, c, big, cc, kc, ginv)

    top = TOP + SKIP
    for at in range(LAYERS):
        two[at + 1, top : top + INNER, :] = middle(one, at + 1, INNER, top) / middle(g, at + 1, INNER, top)
    row_at = SKIP + lax.broadcasted_iota(jnp.int32, (INNER, LANES), 0)
    lane = lanes_of((INNER, LANES))
    across = row_at + (lax.axis_index("au") * OWN - HALO)
    along = lane + (lax.axis_index("vert") * (8 * PART) + lax.axis_index("row") * PART - MARGIN)
    own = (row_at >= HALO) & (row_at < HALO + OWN) & (lane >= MARGIN) & (lane < MARGIN + PART)
    shares = [
        jnp.where(edge, 1.0, 0.5)
        for edge in (
            across == 0,
            across == lax.axis_size("au") * OWN - 1,
            along == 0,
            along == lax.axis_size("vert") * 8 * PART - 1,
        )
    ]
    column = jnp.zeros((INNER, LANES), F32)
    for at in range(LAYERS):
        g_mid, *g_four = four(g, at + 1, INNER, 1, top)
        v_mid, *v_four = four(vel, at + 1, INNER, 1, top)
        x_mid, *x_four = four(two, at + 1, INNER, 1, top)
        total = jnp.zeros((INNER, LANES), F32)
        for share, g_n, v_n, x_n in zip(shares, g_four, v_four, x_four):
            total = total + (share * g_n) * ((x_n - x_mid) * (v_n - v_mid))
        for other, end in ((at, 0), (at + 2, LAYERS + 1)):
            share = 1.0 if other == end else 0.5
            x_n, v_n = middle(two, other, INNER, top), middle(vel, other, INNER, top)
            total = total + (share * middle(g, other, INNER, top)) * ((x_n - x_mid) * (v_n - v_mid))
        total = jnp.where(own, g_mid * total, 0.0)
        column = column + tall(depth_at(at), INNER) * total
        layers[at] = jnp.sum(total.reshape(INNER // 8, 8, LANES), axis=0)
    level = jnp.sum(layers[...], axis=1)

    high = label_window[...] >> 7
    sums = column[HALO - SKIP : HALO - SKIP + OWN, :]
    kind = lax.broadcasted_iota(jnp.int32, (4, LANES), 0)
    left = []
    for at in range(OWN):
        value = jnp.where(high[at : at + 1, :] == kind, sums[at : at + 1, :], 0.0)
        first = value.astype(jnp.bfloat16).astype(F32)
        rest = value - first
        then = rest.astype(jnp.bfloat16).astype(F32)
        left.append(jnp.concatenate([first, then, rest - then, jnp.zeros_like(first)], axis=0).astype(jnp.bfloat16))
    product = lax.dot_general(
        jnp.concatenate(left, axis=1), ones[...], (((1,), (1,)), ((), ())), preferred_element_type=F32
    )
    segments = (product[0:4] + product[4:8]) + product[8:12]

    slot = lanes_of((OWN, LANES)) // PART
    for part in range(8):
        tile = turn(two[4 * part + 1, TOP + HALO : TOP + HALO + OWN, :], -MARGIN)
        for row in range(1, 4):
            x = two[4 * part + row + 1, TOP + HALO : TOP + HALO + OWN, :]
            tile = jnp.where(slot == row, turn(x, PART * row - MARGIN), tile)
        send[part, 0:16, :] = inc[part]
        send[part, 16:32, :] = tile
        send[part, 32:36, :] = segments
        send[part, 36:40, :] = level[4 * part : 4 * part + 4, :]


def place_kernel(got, inc, adj, spread):
    lane = lanes_of((OWN, LANES))
    slot = lane // PART
    for out, start in ((inc, 0), (adj, 16)):
        for row in range(4):
            for half in range(2):
                tile = jnp.zeros((OWN, LANES), F32)
                for source in range(4):
                    piece = got[4 * half + source, start : start + 16, :]
                    tile = jnp.where(slot == source, turn(piece, PART * (source - row)), tile)
                out[row, :, half * LANES : (half + 1) * LANES] = tile
    total = got[0, 32:40, :]
    for source in range(1, 8):
        total = total + got[source, 32:40, :]
    level = jnp.zeros((1, LANES), F32)
    lane = lanes_of((1, LANES))
    for row in range(4):
        level = jnp.where(lane == row, jnp.sum(total[4 + row : 5 + row, :], axis=1, keepdims=True), level)
    pieces = [total[row : row + 1, :] for row in range(4)] + [level]
    line = jnp.concatenate(pieces, axis=1)
    for other in range(spread.shape[0]):
        spread[other] = line


def total_kernel(parts, segments, layers):
    cells = LAYERS * lax.axis_size("au") * OWN * lax.axis_size("vert") * 8 * PART
    total = jnp.sum(parts[...], axis=0)
    for row in range(4):
        segments[row : row + 1, :] = total[:, row * LANES : (row + 1) * LANES] * (1.0 / (cells / NSEG) ** 0.5)
    layers[...] = total[:, 4 * LANES : 4 * LANES + 4] * (1.0 / (cells / LAYERS) ** 0.5)


def shards(velocity, log_visc, labels, seg_dir, layer_dir):
    vert = lax.axis_size("vert")
    across = lax.axis_size("au")
    ahead = [(i, (i + 1) % vert) for i in range(vert)]
    back = [((i + 1) % vert, i) for i in range(vert)]
    upward = [(i, i + 1) for i in range(across - 1)]
    downward = [(i + 1, i) for i in range(across - 1)]
    vmem = pl.BlockSpec(memory_space=pltpu.VMEM)
    hbm = pl.BlockSpec(memory_space=pltpu.HBM)
    labels_like = jax.ShapeDtypeStruct((OWN, 2 * LANES), jnp.int32)
    label_tile = jax.ShapeDtypeStruct((OWN, LANES), jnp.int32)
    edges, field = sds(3, OWN, LANES), sds(4, OWN, 2 * LANES)

    left, right, plate, vel, log, lab = call(
        edge_kernel,
        (edges, edges, sds(OWN, 2 * LANES), field, field, labels_like),
        [pltpu.VMEM((4, LANES), F32), pltpu.SemaphoreType.DMA((4,))],
        in_specs=[hbm] * 4,
        limit=EDGE_LIMIT,
    )(velocity, log_visc, labels, seg_dir.reshape(4, LANES))
    from_left = lax.ppermute(right, "vert", ahead)
    from_right = lax.ppermute(left, "vert", back)
    send = call(
        window_kernel,
        sds(8, 5, OWN, LANES),
        in_specs=[vmem, vmem, pl.BlockSpec(memory_space=pltpu.SMEM)],
    )(vel, log, layer_dir)
    send, plate_window, label_window = call(
        patch_kernel, (sds(8, 5, OWN, LANES), sds(OWN, LANES), label_tile)
    )(send, plate, lab, left, right, from_left, from_right)
    got = lax.all_to_all(send, "row", 0, 0, tiled=True)
    up, down = call(rows_kernel, (sds(62, 8, LANES), sds(62, 8, LANES)))(got, plate_window)
    from_low = lax.ppermute(up, "au", upward)
    from_high = lax.ppermute(down, "au", downward)
    fine = sds(LAYERS, WINDOW, LANES)
    fine_padded = sds(LAYERS + 2, PAD_ROWS, LANES)
    coarse = sds(LAYERS // 2, HALF, LANES)
    own = sds(LAYERS, OWN, LANES)
    fine_scratch = pltpu.VMEM((LAYERS + 2, PAD_ROWS, LANES), F32)
    coarse_scratch = pltpu.VMEM((LAYERS // 2 + 2, HALF_ROWS, LANES), F32)
    spare = pltpu.VMEM((LAYERS // 2, WINDOW, LANES), F32)
    *factors, x_own, f_own, f_up, f_down = call(
        first_kernel,
        (fine_padded, fine, fine, coarse, coarse, coarse, fine_padded)
        + (own, sds(LAYERS // 2, OWN, LANES), sds(24, 8, LANES), sds(24, 8, LANES)),
        [pltpu.VMEM((TILES + 1, WINDOW, LANES), F32)]
        + [fine_scratch] * 3
        + [coarse_scratch] * 3
        + [spare, pltpu.VMEM((LAYERS + 2, 8, LANES), F32), coarse_scratch],
    )(got, plate_window, from_low, from_high)
    from_low = lax.ppermute(f_up, "au", upward)
    from_high = lax.ppermute(f_down, "au", downward)
    inc, ones = call(
        side_kernel, (sds(8, OWN, LANES), jax.ShapeDtypeStruct((LANES, OWN * LANES), jnp.bfloat16))
    )(x_own, label_window)
    send = call(
        second_kernel,
        sds(8, 40, LANES),
        [fine_scratch] * 3 + [coarse_scratch] * 3 + [spare, pltpu.VMEM((LAYERS, 8, LANES), F32)],
    )(*factors, f_own, from_low, from_high, inc, label_window, ones)
    got = lax.all_to_all(send, "row", 0, 0, tiled=True)
    increment, adjoint, spread = call(place_kernel, (field, field, sds(across * vert, 1, 5 * LANES)))(got)
    parts = lax.all_to_all(spread, ("au", "vert"), 0, 0, tiled=True)
    hv_segments, hv_layers = call(total_kernel, (sds(4, LANES), sds(1, 4)))(parts)
    return increment, adjoint, hv_segments.reshape(NSEG), hv_layers.reshape(4)


def solution(mesh):
    in_specs = (P("row", "au", "vert"), P("row", "au", "vert"), P("au", "vert"), P(), P("row"))
    out_specs = (P("row", "au", "vert"), P("row", "au", "vert"), P(), P("row"))
    return jax.shard_map(shards, mesh=mesh, in_specs=in_specs, out_specs=out_specs, check_vma=False)
```

```python
import jax
import jax.numpy as jnp
from jax import lax
from jax.experimental import pallas as pl
from jax.experimental.pallas import tpu as pltpu
from jax.sharding import PartitionSpec as P

NSEG = 512
DAMPING = 0.7
KEEP = 1.0 - DAMPING
COARSE_FACTOR = 0.25

LAYERS = 32
OWN = 16
HALO = 12
WINDOW = OWN + 2 * HALO
PART = 32
MARGIN = 24
SPAN = PART + 2 * MARGIN
LANES = 128
TOP = 8
HALF = WINDOW // 2
HALF_ROWS = 40
INNER = 24
SKIP = 8
NARROW = 8
PAD_ROWS = WINDOW + 2 * TOP
TILES = 40
F32 = jnp.float32
VMEM_LIMIT = 24 * 1024 * 1024
EDGE_LIMIT = 56360000


def lanes_of(shape):
    return lax.broadcasted_iota(jnp.int32, shape, len(shape) - 1)


def turn(values, amount):
    return pltpu.roll(values, amount % LANES, values.ndim - 1)


def call(kernel, outs, scratch=(), limit=VMEM_LIMIT, **more):
    return pl.pallas_call(
        kernel,
        out_shape=outs,
        **more,
        scratch_shapes=list(scratch),
        compiler_params=pltpu.CompilerParams(vmem_limit_bytes=limit),
    )


def sds(*shape):
    return jax.ShapeDtypeStruct(shape, F32)


def edge_kernel(vel_in, log_in, left, right, vel, log, sems):
    copies = [
        pltpu.make_async_copy(source, target, sems.at[number])
        for number, (source, target) in enumerate(((vel_in, vel), (log_in, log)))
    ]
    for copy in copies:
        copy.start()
    for copy in copies:
        copy.wait()
    slot = lanes_of((OWN, LANES)) // PART
    for group, field in enumerate((vel, log)):
        first = field[0, :, 0:LANES]
        last = turn(field[0, :, LANES : 2 * LANES], MARGIN)
        for row in range(1, 4):
            first = jnp.where(slot == row, turn(field[row, :, 0:LANES], PART * row), first)
            last = jnp.where(slot == row, turn(field[row, :, LANES : 2 * LANES], PART * row + MARGIN), last)
        left[group] = first
        right[group] = last


def plate_kernel(lab, seg, plate, left, right, label_window):
    for top in (0, 8):
        for half in range(2):
            labels = lab[top : top + 8, half * LANES : (half + 1) * LANES]
            low = labels & 127
            high = labels >> 7
            value = jnp.zeros((8, LANES), F32)
            for part in range(4):
                table = jnp.broadcast_to(seg[part : part + 1, :], (8, LANES))
                got = jnp.take_along_axis(table, low, axis=1, mode="promise_in_bounds")
                value = jnp.where(high == part, got, value)
            plate[top : top + 8, half * LANES : (half + 1) * LANES] = value
    left[...] = plate[:, 0:LANES]
    right[...] = turn(plate[:, LANES : 2 * LANES], MARGIN)
    part = lax.axis_index("row")
    labels = jnp.where(part >= 4, lab[:, LANES : 2 * LANES], lab[:, 0:LANES])
    label_window[...] = pltpu.roll(labels, (LANES + MARGIN - NARROW - PART * (part % 4)) % LANES, 1)


PIECES = (
    ((0, 0, 0, 80),),
    ((1, 0, 0, 80),),
    ((2, 0, 0, 80),),
    ((3, 0, 0, 80),),
    ((4, 0, 0, 80),),
    ((0, 80, 0, 48), (1, 80, 48, 32)),
    ((1, 112, 0, 16), (2, 80, 16, 48), (3, 80, 64, 16)),
    ((3, 96, 0, 32), (4, 80, 32, 48)),
)


def window_kernel(vel, log, layer, send):
    lane = lanes_of((OWN, LANES))
    turned = {}

    def at(slab, half, amount):
        key = (slab, half, amount % LANES)
        if key not in turned:
            field = (vel, log)[slab // 4]
            turned[key] = turn(field[slab % 4, :, half * LANES : (half + 1) * LANES], amount)
        return turned[key]

    for part in range(8):
        tiles = [None] * 5
        for slab, pieces in enumerate(PIECES):
            for tile, start, first, count in pieces:
                shift = start - first
                amount = MARGIN - PART * part + shift
                edge = LANES + MARGIN - PART * part + shift
                if edge >= start + count:
                    wide = at(slab, 0, amount)
                elif edge <= start:
                    wide = at(slab, 1, amount)
                else:
                    wide = jnp.where(lane < edge, at(slab, 0, amount), at(slab, 1, amount))
                if slab < 4:
                    wide = jnp.where(lane == SPAN - 1, layer[slab], wide)
                if tiles[tile] is None:
                    tiles[tile] = wide
                else:
                    tiles[tile] = jnp.where((lane >= start) & (lane < start + count), wide, tiles[tile])
        for tile in range(5):
            send[part, tile] = tiles[tile]


def inner(edge, own, group, low):
    place = lanes_of((OWN, LANES)) % PART
    near, next_one = (MARGIN - 1, MARGIN - 2) if low else (0, 1)
    if group == 0:
        return jnp.where((place == near) | (place == next_one), 0.0, edge)
    sign = 1 if low else -1
    edge = jnp.where(place == near, turn(own, sign * (MARGIN - 1)), edge)
    return jnp.where(place == next_one, turn(own, sign * (MARGIN - 3)), edge)


def patch_kernel(sent, left, right, from_left, from_right, send):
    lane = lanes_of((OWN, LANES))
    first = lax.axis_index("vert") == 0
    last = lax.axis_index("vert") == lax.axis_size("vert") - 1
    before, after = [], []
    for group in range(2):
        low, high = from_left[group], from_right[group]
        before.append(jnp.where(first, inner(low, left[group], group, True), low))
        after.append(jnp.where(last, inner(high, right[group], group, False), high))
    for part in range(1, 7):
        send[part] = sent[part]
    for part, edges, begin, stop in ((0, before, 0, MARGIN), (7, after, SPAN - MARGIN, SPAN)):
        tiles = [sent[part, tile] for tile in range(5)]
        for slab, pieces in enumerate(PIECES):
            group, row = slab // 4, slab % 4
            end = SPAN - 1 if group == 0 and stop == SPAN else stop
            for tile, start, head, count in pieces:
                low, high = max(begin, head), min(end, head + count)
                if low >= high:
                    continue
                shift = start - head
                moved = turn(edges[group], shift + begin - PART * row)
                tiles[tile] = jnp.where((lane >= low + shift) & (lane < high + shift), moved, tiles[tile])
        for tile in range(5):
            send[part, tile] = tiles[tile]


def rows_kernel(got, plate, left, right, from_left, from_right, up, down, plate_window):
    lane = lanes_of((OWN, LANES))
    first = lax.axis_index("vert") == 0
    last = lax.axis_index("vert") == lax.axis_size("vert") - 1
    before = jnp.where(first, inner(from_left[...], left[...], 1, True), from_left[...])
    after = jnp.where(last, inner(from_right[...], right[...], 1, False), from_right[...])
    part = lax.axis_index("row")
    shift = PART * (part % 4)
    one, two = turn(plate[:, 0:LANES], MARGIN), turn(plate[:, LANES : 2 * LANES], MARGIN)
    head = lane < MARGIN
    tiles = (jnp.where(head, before, one), jnp.where(head, one, two), jnp.where(head, two, turn(after, MARGIN)))
    late = part >= 4
    here = jnp.where(late, tiles[1], tiles[0])
    there = jnp.where(late, tiles[2], tiles[1])
    back = (LANES - shift) % LANES
    window = jnp.where(lane < LANES - shift, pltpu.roll(here, back, 1), pltpu.roll(there, back, 1))
    plate_window[...] = window
    for index in range(TILES + 1):
        values = got[index // 5, index % 5] if index < TILES else window
        at = TILES + 1 + index // 2
        half = 4 * (index % 2)
        up[index] = values[8:16]
        down[index] = values[0:8]
        up[at, half : half + 4, :] = values[4:8]
        down[at, half : half + 4, :] = values[8:12]


def rows_of(index, up, down, total):
    at = total + index // 2
    half = 4 * (index % 2)
    return up[at, half : half + 4, :], up[index], down[index], down[at, half : half + 4, :]


def places(rows=WINDOW):
    step = WINDOW // rows
    row_at = lax.broadcasted_iota(jnp.int32, (rows, LANES), 0)
    lane = lanes_of((rows, LANES))
    across = step * row_at + (lax.axis_index("au") * OWN - HALO)
    along = lane + (lax.axis_index("vert") * (8 * PART) + lax.axis_index("row") * PART - MARGIN)
    across_end = lax.axis_size("au") * OWN
    along_end = lax.axis_size("vert") * 8 * PART
    domain = (across >= 0) & (across < across_end) & (along >= 0) & (along < along_end) & (lane < SPAN)
    return row_at, lane, across, along, across_end, along_end, domain


def middle(ref, at, rows=WINDOW, top=TOP):
    return ref[at, top : top + rows, :]


def four(ref, at, rows=WINDOW, reach=1, top=TOP):
    centre = middle(ref, at, rows, top)
    return (
        centre,
        ref[at, top - 1 : top - 1 + rows, :],
        ref[at, top + 1 : top + 1 + rows, :],
        turn(centre, reach),
        turn(centre, -reach),
    )


def around(ref, at, rows=WINDOW, reach=1, top=TOP):
    centre, low, high, left, right = four(ref, at, rows, reach, top)
    total = (low + high) + (left + right)
    return centre, total + (middle(ref, at - 1, rows, top) + middle(ref, at + 1, rows, top))


def pair_sum(spare, even_lane):
    total = spare[pl.ds(0, HALF, 2), :] + spare[pl.ds(1, HALF, 2), :]
    return total + jnp.where(even_lane, turn(total, -1), turn(total, 1))


def clear_edges(refs, rows=WINDOW, skip=0):
    row = jnp.zeros((1, LANES), F32)
    slab = jnp.zeros((rows, LANES), F32)
    top = TOP + skip
    for ref in refs:
        last = ref.shape[0] - 1
        for at in range(1, last):
            ref[at, top - 1 : top, :] = row
            ref[at, top + rows : top + rows + 1, :] = row
        ref[0, top : top + rows, :] = slab
        ref[last, top : top + rows, :] = slab


def join(ref, rows=WINDOW, skip=0):
    top = TOP + skip
    last = ref.shape[0] - 2
    low = lanes_of((rows, LANES)) < 64
    ref[0, top : top + rows, :] = jnp.where(low, 0.0, turn(middle(ref, last, rows, top), 64))
    ref[last + 1, top : top + rows, :] = jnp.where(low, turn(middle(ref, 1, rows, top), 64), 0.0)


def smooth(out, values, source, factor, rows=WINDOW, reach=1, skip=0):
    top = TOP + skip
    for at in range(out.shape[0] - 2):
        centre, total = around(values, at + 1, rows, reach, top)
        if source is None:
            result = (1.0 + KEEP) * centre
        else:
            result = KEEP * centre + middle(source, at + 1, rows, top)
        out[at + 1, top : top + rows, :] = result + factor[at, skip : skip + rows, :] * total


def vcycle(f, one, two, zf, za, zb, spare, g, g_top, c, big, cc, kc, ginv, joined):
    even_lane = lanes_of((HALF, LANES)) % 2 == 0
    count = zf.shape[0] - 2

    def close(ref, rows=WINDOW, skip=0):
        if joined:
            join(ref, rows, skip)

    smooth(two, f, None, c)
    close(two)

    def leftover(at):
        centre, total = around(two, at + 1)
        return big[at] * ((middle(f, at + 1) - DAMPING * centre) + c[at] * total)

    for at in range(count):
        spare[at] = leftover(2 * at) + leftover(2 * at + 1)
    for at in range(count):
        zf[at + 1, TOP : TOP + HALF, :] = kc[at] * pair_sum(spare.at[at], even_lane)
    close(zf, HALF)
    smooth(za, zf, None, cc, HALF, 2)
    close(za, HALF)
    smooth(zb, za, zf, cc, HALF, 2)
    close(zb, HALF)
    smooth(za, zb, zf, cc, 16, 2)
    for at in range(count):
        value = middle(za, at + 1, 16) * ginv[at, 0:16, :]
        spare[at, pl.ds(0, 16, 2), :] = value
        spare[at, pl.ds(1, 16, 2), :] = value
    top = TOP + SKIP
    for at in range(count):
        value = spare[at, SKIP : SKIP + INNER, :]
        for row in (2 * at + 1, 2 * at + 2):
            one[row, top : top + INNER, :] = (
                middle(two, row, INNER, top) + middle(g, row, INNER, g_top + SKIP) * value
            )
    close(one, INNER, SKIP)
    smooth(two, one, f, c, INNER, 1, SKIP)
    close(two, INNER, SKIP)
    smooth(one, two, f, c, INNER, 1, SKIP)


def depth_at(at):
    place = jnp.zeros((8, LANES), jnp.int32) + at
    return jnp.exp(-(LAYERS - 1 - place).astype(F32) / (LAYERS / 4.0))


def tall(values, rows=WINDOW):
    return jnp.concatenate([values] * (rows // 8), axis=0)


def first_kernel(
    got, plate_window, from_low, from_high,
    g, c, big, cc, kc, ginv, vel, x_own, f_own, f_up, f_down,
    packed, f, one, two, zf, za, zb, spare, layer, gc,
):
    domain = places()[-1]
    coarse_domain = places(HALF)[-1]
    clear_edges((f, two, vel, g))
    clear_edges((one,), INNER, SKIP)
    clear_edges((zf, za, zb, gc), HALF)
    for index in range(TILES + 1):
        a, b, d, e = rows_of(index, from_low, from_high, TILES + 1)
        packed[index, 0:4, :] = a
        packed[index, 4:12, :] = b
        packed[index, 12:28, :] = got[index // 5, index % 5] if index < TILES else plate_window[...]
        packed[index, 28:36, :] = d
        packed[index, 36:40, :] = e

    def mirror(pairs):
        speed = lanes_of((1, LANES)) < SPAN
        for index in range(TILES + 1):
            for target, source in pairs:
                value = packed[index, source : source + 1, :]
                if index < TILES and index % 5 < 4:
                    value = jnp.where(speed, 0.0, value)
                packed[index, target : target + 1, :] = value

    @pl.when(lax.axis_index("au") == 0)
    def _():
        mirror(((HALO - 1, HALO), (HALO - 2, HALO + 1)))

    @pl.when(lax.axis_index("au") == lax.axis_size("au") - 1)
    def _():
        mirror(((HALO + OWN, HALO + OWN - 1), (HALO + OWN + 1, HALO + OWN - 2)))

    lane = lanes_of((WINDOW, LANES))
    even_lane = lanes_of((HALF, LANES)) % 2 == 0

    def slab_of(source, slab):
        result = jnp.zeros((WINDOW, LANES), F32)
        for tile, start, first, count in reversed(PIECES[slab]):
            result = jnp.where(lane < first + count, turn(packed[source * 5 + tile], first - start), result)
        return result

    for source in range(8):
        logs = []
        for row in range(4):
            at = source * 4 + row + 1
            speed = slab_of(source, row)
            layer[at] = jnp.broadcast_to(speed[16:24, SPAN - 1 : SPAN], (8, LANES))
            vel[at, TOP : TOP + WINDOW, :] = speed
            logs.append(slab_of(source, 4 + row))
            g[at, TOP : TOP + WINDOW, :] = jnp.exp(0.5 * logs[-1])
        for pair in range(2):
            spare[2 * source + pair] = logs[2 * pair] + logs[2 * pair + 1]
    for at in range(LAYERS // 2):
        gc[at + 1, TOP : TOP + HALF, :] = jnp.exp(0.0625 * pair_sum(spare.at[at], even_lane))
    layer[0] = layer[1]
    layer[LAYERS + 1] = layer[LAYERS]
    g[0] = g[1]
    g[LAYERS + 1] = g[LAYERS]
    gc[0] = gc[1]
    gc[LAYERS // 2 + 1] = gc[LAYERS // 2]

    for at in range(LAYERS // 2):
        centre, total = around(gc, at + 1, HALF, 2)
        per = jnp.where(coarse_domain, DAMPING / total, 0.0)
        cc[at] = centre * per
        kc[at] = (0.125 / COARSE_FACTOR) * per
        ginv[at] = 1.0 / centre

    plate = packed[TILES]
    two[1, TOP : TOP + WINDOW, :] = plate
    beside = [plate + other for other in four(two, 1)[1:]]
    across_layers = None
    for at in range(LAYERS):
        g_mid, *g_four = four(g, at + 1)
        v_mid, *v_four = four(vel, at + 1)
        depth = depth_at(at)
        level = layer[at + 1]
        depth_tall, twice = tall(depth), tall(2.0 * level)
        total_g = (g_four[0] + g_four[1]) + (g_four[2] + g_four[3])
        total_g = total_g + (middle(g, at) + middle(g, at + 2))
        total = jnp.zeros((WINDOW, LANES), F32)
        for g_n, v_n, s_n in zip(g_four, v_four, beside):
            total = total + g_n * (depth_tall * s_n + twice) * (v_mid - v_n)
        total = g_mid * total
        for other in (at, at + 2):
            place = min(max(other - 1, 0), LAYERS - 1)
            if other == at and at > 0:
                total = total - across_layers
                continue
            scale = tall(depth + depth_at(place)) * plate + tall(level + layer[other])
            across_layers = (g_mid * middle(g, other)) * scale * (v_mid - middle(vel, other))
            total = total + across_layers
        per = jnp.where(domain, DAMPING / total_g, 0.0)
        c[at] = g_mid * per
        big[at] = total_g * (1.0 / DAMPING)
        f[at + 1, TOP : TOP + WINDOW, :] = -0.5 * total * per
    vcycle(f, one, two, zf, za, zb, spare, g, TOP, c, big, cc, kc, ginv, False)

    own_lane = lanes_of((OWN, LANES))
    sent = []
    for at in range(LAYERS):
        ratio = 1.0 / g[at + 1, TOP + HALO : TOP + HALO + OWN, :]
        x = one[at + 1, TOP + HALO : TOP + HALO + OWN, :] * ratio
        x_own[at] = x
        sent.append(-(x * (c[at, HALO : HALO + OWN, :] * ratio)))
    for index in range(16):
        both = jnp.where(own_lane < 64, turn(sent[index], -NARROW), turn(sent[index + 16], 64 - NARROW))
        start = 4 * (index % 2)
        f_own[index] = both
        f_up[index] = both[8:16]
        f_down[index] = both[0:8]
        f_up[16 + index // 2, start : start + 4, :] = both[4:8]
        f_down[16 + index // 2, start : start + 4, :] = both[8:12]


def side_kernel(
    g, c, big, cc, kc, ginv, vel, x_own, label_window,
    inc, ones, g_two, c_two, big_two, cc_two, kc_two, ginv_two, vel_two,
):
    slot = lanes_of((OWN, LANES)) // PART
    for part in range(8):
        tile = turn(x_own[4 * part], -MARGIN)
        for row in range(1, 4):
            tile = jnp.where(slot == row, turn(x_own[4 * part + row], PART * row - MARGIN), tile)
        inc[part] = tile
    low = label_window[...] & 127
    place = lax.broadcasted_iota(jnp.int32, (LANES, LANES), 0)
    for at in range(OWN):
        hit = jnp.where(low[at : at + 1, :] == place, 1.0, 0.0)
        ones[:, at * LANES : (at + 1) * LANES] = hit.astype(jnp.bfloat16)
    for source, target in ((g, g_two), (vel, vel_two), (c, c_two), (big, big_two), (cc, cc_two), (kc, kc_two), (ginv, ginv_two)):
        rows = target.shape[1]
        top = TOP if source.shape[1] == PAD_ROWS else 0
        first = lanes_of((rows, LANES)) < 64
        for at in range(target.shape[0]):
            upper = at + (8 if rows == HALF else 16)
            target[at] = jnp.where(
                first, turn(middle(source, at, rows, top), -NARROW), turn(middle(source, upper, rows, top), 64 - NARROW)
            )


def second_kernel(
    g, c, big, cc, kc, ginv, vel, f_own, from_low, from_high, inc, label_window, ones,
    send,
    f, one, two, zf, za, zb, spare, layers,
):
    count = LAYERS // 2
    clear_edges((f, two))
    clear_edges((one,), INNER, SKIP)
    clear_edges((zf, za, zb), HALF)
    for index in range(count):
        start = 4 * (index % 2)
        at = index + 1
        f[at, TOP : TOP + 4, :] = from_low[16 + index // 2, start : start + 4, :]
        f[at, TOP + 4 : TOP + 12, :] = from_low[index]
        f[at, TOP + HALO : TOP + HALO + OWN, :] = f_own[index]
        f[at, TOP + 28 : TOP + 36, :] = from_high[index]
        f[at, TOP + 36 : TOP + 40, :] = from_high[16 + index // 2, start : start + 4, :]
    join(f)
    vcycle(f, one, two, zf, za, zb, spare, g, 0, c, big, cc, kc, ginv, True)

    top = TOP + SKIP
    for at in range(count):
        two[at + 1, top : top + INNER, :] = middle(one, at + 1, INNER, top) / middle(g, at + 1, INNER, SKIP)
    join(two, INNER, SKIP)
    row_at = SKIP + lax.broadcasted_iota(jnp.int32, (INNER, LANES), 0)
    lane = lanes_of((INNER, LANES))
    low = lane < 64
    place = lane % 64 + NARROW
    across = row_at + (lax.axis_index("au") * OWN - HALO)
    along = place + (lax.axis_index("vert") * (8 * PART) + lax.axis_index("row") * PART - MARGIN)
    own = (row_at >= HALO) & (row_at < HALO + OWN) & (place >= MARGIN) & (place < MARGIN + PART)
    shares = [
        jnp.where(edge, 1.0, 0.5)
        for edge in (
            across == 0,
            across == lax.axis_size("au") * OWN - 1,
            along == 0,
            along == lax.axis_size("vert") * 8 * PART - 1,
        )
    ]
    column = jnp.zeros((INNER, LANES), F32)
    upper = (lanes_of((8, LANES)) >= 64).astype(jnp.int32) * count
    for at in range(count):
        g_mid, *g_four = four(g, at + 1, INNER, 1, SKIP)
        v_mid, *v_four = four(vel, at + 1, INNER, 1, SKIP)
        x_mid, *x_four = four(two, at + 1, INNER, 1, top)
        total = jnp.zeros((INNER, LANES), F32)
        for share, g_n, v_n, x_n in zip(shares, g_four, v_four, x_four):
            total = total + (share * g_n) * ((x_n - x_mid) * (v_n - v_mid))
        for other in (at, at + 2):
            share = 0.5
            if other == 0:
                share = jnp.where(low, 1.0, 0.5)
            if other == count + 1:
                share = jnp.where(low, 0.5, 1.0)
            x_n, v_n = middle(two, other, INNER, top), middle(vel, other, INNER, SKIP)
            total = total + (share * middle(g, other, INNER, SKIP)) * ((x_n - x_mid) * (v_n - v_mid))
        total = jnp.where(own, g_mid * total, 0.0)
        column = column + tall(depth_at(upper + at), INNER) * total
        layers[at] = jnp.sum(total.reshape(INNER // 8, 8, LANES), axis=0)
    level = jnp.sum(layers[...], axis=1)

    high = label_window[...] >> 7
    column = jnp.where(low, column + turn(column, 64), 0.0)
    sums = column[HALO - SKIP : HALO - SKIP + OWN, :]
    kind = lax.broadcasted_iota(jnp.int32, (4, LANES), 0)
    left = []
    for at in range(OWN):
        value = jnp.where(high[at : at + 1, :] == kind, sums[at : at + 1, :], 0.0)
        first = value.astype(jnp.bfloat16).astype(F32)
        rest = value - first
        then = rest.astype(jnp.bfloat16).astype(F32)
        left.append(jnp.concatenate([first, then, rest - then, jnp.zeros_like(first)], axis=0).astype(jnp.bfloat16))
    product = lax.dot_general(
        jnp.concatenate(left, axis=1), ones[...], (((1,), (1,)), ((), ())), preferred_element_type=F32
    )
    segments = (product[0:4] + product[4:8]) + product[8:12]

    slot = lanes_of((OWN, LANES)) // PART
    lower = lanes_of((4, LANES)) < 64
    for part in range(8):
        half, at = part // 4, 4 * (part % 4)
        tile = None
        for row in range(4):
            x = two[at + row + 1, TOP + HALO : TOP + HALO + OWN, :]
            x = turn(x, PART * row - (MARGIN - NARROW) - 64 * half)
            tile = x if tile is None else jnp.where(slot == row, x, tile)
        send[part, 0:16, :] = inc[part]
        send[part, 16:32, :] = tile
        send[part, 32:36, :] = segments
        here = level[at : at + 4, :]
        send[part, 36:40, :] = jnp.where(lower, 0.0, here) if half else jnp.where(lower, here, 0.0)


def sum_kernel(got, spread):
    total = got[0, 32:40, :]
    for source in range(1, 8):
        total = total + got[source, 32:40, :]
    level = jnp.zeros((1, LANES), F32)
    lane = lanes_of((1, LANES))
    for row in range(4):
        level = jnp.where(lane == row, jnp.sum(total[4 + row : 5 + row, :], axis=1, keepdims=True), level)
    pieces = [total[row : row + 1, :] for row in range(4)] + [level]
    line = jnp.concatenate(pieces, axis=1)
    for other in range(spread.shape[0]):
        spread[other] = line


def place_kernel(got, parts, inc, adj, segments, layers):
    lane = lanes_of((OWN, LANES))
    slot = lane // PART
    for out, start in ((inc, 0), (adj, 16)):
        for row in range(4):
            for half in range(2):
                tile = jnp.zeros((OWN, LANES), F32)
                for source in range(4):
                    piece = got[4 * half + source, start : start + 16, :]
                    tile = jnp.where(slot == source, turn(piece, PART * (source - row)), tile)
                out[row, :, half * LANES : (half + 1) * LANES] = tile
    cells = LAYERS * lax.axis_size("au") * OWN * lax.axis_size("vert") * 8 * PART
    total = jnp.sum(parts[...], axis=0)
    for row in range(4):
        segments[row : row + 1, :] = total[:, row * LANES : (row + 1) * LANES] * (1.0 / (cells / NSEG) ** 0.5)
    layers[...] = total[:, 4 * LANES : 4 * LANES + 4] * (1.0 / (cells / LAYERS) ** 0.5)


def shards(velocity, log_visc, labels, seg_dir, layer_dir):
    vert = lax.axis_size("vert")
    across = lax.axis_size("au")
    ahead = [(i, (i + 1) % vert) for i in range(vert)]
    back = [((i + 1) % vert, i) for i in range(vert)]
    upward = [(i, i + 1) for i in range(across - 1)]
    downward = [(i + 1, i) for i in range(across - 1)]
    vmem = pl.BlockSpec(memory_space=pltpu.VMEM)
    hbm = pl.BlockSpec(memory_space=pltpu.HBM)
    label_tile = jax.ShapeDtypeStruct((OWN, LANES), jnp.int32)
    tile, pair, field = sds(OWN, LANES), sds(2, OWN, LANES), sds(4, OWN, 2 * LANES)

    left, right, vel, log = call(
        edge_kernel,
        (pair, pair, field, field),
        [pltpu.SemaphoreType.DMA((2,))],
        in_specs=[hbm] * 2,
        limit=EDGE_LIMIT,
    )(velocity, log_visc)
    from_left = lax.ppermute(right, "vert", ahead)
    from_right = lax.ppermute(left, "vert", back)
    plate, plate_left, plate_right, label_window = call(
        plate_kernel, (sds(OWN, 2 * LANES), tile, tile, label_tile)
    )(labels, seg_dir.reshape(4, LANES))
    plate_before = lax.ppermute(plate_right, "vert", ahead)
    plate_after = lax.ppermute(plate_left, "vert", back)
    send = call(
        window_kernel,
        sds(8, 5, OWN, LANES),
        in_specs=[vmem, vmem, pl.BlockSpec(memory_space=pltpu.SMEM)],
    )(vel, log, layer_dir)
    send = call(patch_kernel, sds(8, 5, OWN, LANES))(send, left, right, from_left, from_right)
    got = lax.all_to_all(send, "row", 0, 0, tiled=True)
    up, down, plate_window = call(rows_kernel, (sds(62, 8, LANES), sds(62, 8, LANES), tile))(
        got, plate, plate_left, plate_right, plate_before, plate_after
    )
    from_low = lax.ppermute(up, "au", upward)
    from_high = lax.ppermute(down, "au", downward)
    fine = sds(LAYERS, WINDOW, LANES)
    fine_padded = sds(LAYERS + 2, PAD_ROWS, LANES)
    coarse = sds(LAYERS // 2, HALF, LANES)

    def scratch(layers):
        return (
            [pltpu.VMEM((layers + 2, PAD_ROWS, LANES), F32)] * 3
            + [pltpu.VMEM((layers // 2 + 2, HALF_ROWS, LANES), F32)] * 3
            + [pltpu.VMEM((layers // 2, WINDOW, LANES), F32)]
        )

    *factors, x_own, f_own, f_up, f_down = call(
        first_kernel,
        (fine_padded, fine, fine, coarse, coarse, coarse, fine_padded)
        + (sds(LAYERS, OWN, LANES), sds(LAYERS // 2, OWN, LANES), sds(24, 8, LANES), sds(24, 8, LANES)),
        [pltpu.VMEM((TILES + 1, WINDOW, LANES), F32)]
        + scratch(LAYERS)
        + [pltpu.VMEM((LAYERS + 2, 8, LANES), F32), pltpu.VMEM((LAYERS // 2 + 2, HALF_ROWS, LANES), F32)],
    )(got, plate_window, from_low, from_high)
    from_low = lax.ppermute(f_up, "au", upward)
    from_high = lax.ppermute(f_down, "au", downward)
    fine = sds(LAYERS // 2, WINDOW, LANES)
    fine_closed = sds(LAYERS // 2 + 2, WINDOW, LANES)
    coarse = sds(LAYERS // 4, HALF, LANES)
    inc, ones, *factors = call(
        side_kernel,
        (sds(8, OWN, LANES), jax.ShapeDtypeStruct((LANES, OWN * LANES), jnp.bfloat16))
        + (fine_closed, fine, fine, coarse, coarse, coarse, fine_closed),
    )(*factors, x_own, label_window)
    send = call(second_kernel, sds(8, 40, LANES), scratch(LAYERS // 2) + [pltpu.VMEM((LAYERS // 2, 8, LANES), F32)])(
        *factors, f_own, from_low, from_high, inc, label_window, ones
    )
    got = lax.all_to_all(send, "row", 0, 0, tiled=True)
    spread = call(sum_kernel, sds(across * vert, 1, 5 * LANES))(got)
    parts = lax.all_to_all(spread, ("au", "vert"), 0, 0, tiled=True)
    increment, adjoint, hv_segments, hv_layers = call(place_kernel, (field, field, sds(4, LANES), sds(1, 4)))(
        got, parts
    )
    return increment, adjoint, hv_segments.reshape(NSEG), hv_layers.reshape(4)


def solution(mesh):
    in_specs = (P("row", "au", "vert"), P("row", "au", "vert"), P("au", "vert"), P(), P("row"))
    out_specs = (P("row", "au", "vert"), P("row", "au", "vert"), P(), P("row"))
    return jax.shard_map(shards, mesh=mesh, in_specs=in_specs, out_specs=out_specs, check_vma=False)
```

```python
import jax
import jax.numpy as jnp
from jax import lax
from jax.experimental import pallas as pl
from jax.experimental.pallas import tpu as pltpu
from jax.sharding import PartitionSpec as P

NSEG = 512
DAMPING = 0.7
KEEP = 1.0 - DAMPING
COARSE_FACTOR = 0.25

LAYERS = 32
OWN = 16
HALO = 12
WINDOW = OWN + 2 * HALO
PART = 32
MARGIN = 24
SPAN = PART + 2 * MARGIN
LANES = 128
TOP = 8
HALF = WINDOW // 2
HALF_ROWS = 40
HALF_TALL = 24
INNER = 24
SKIP = 8
NARROW = 8
PAD_ROWS = WINDOW + 2 * TOP
TILES = 40
F32 = jnp.float32
VMEM_LIMIT = 24 * 1024 * 1024
EDGE_LIMIT = 56360000


def lanes_of(shape):
    return lax.broadcasted_iota(jnp.int32, shape, len(shape) - 1)


def turn(values, amount):
    return pltpu.roll(values, amount % LANES, values.ndim - 1)


def call(kernel, outs, scratch=(), limit=VMEM_LIMIT, **more):
    return pl.pallas_call(
        kernel,
        out_shape=outs,
        **more,
        scratch_shapes=list(scratch),
        compiler_params=pltpu.CompilerParams(vmem_limit_bytes=limit),
    )


def sds(*shape):
    return jax.ShapeDtypeStruct(shape, F32)


def edge_kernel(vel_in, log_in, left, right, vel, log, sems):
    copies = [
        pltpu.make_async_copy(source, target, sems.at[number])
        for number, (source, target) in enumerate(((vel_in, vel), (log_in, log)))
    ]
    for copy in copies:
        copy.start()
    for copy in copies:
        copy.wait()
    slot = lanes_of((OWN, LANES)) // PART
    for group, field in enumerate((vel, log)):
        first = field[0, :, 0:LANES]
        last = turn(field[0, :, LANES : 2 * LANES], MARGIN)
        for row in range(1, 4):
            first = jnp.where(slot == row, turn(field[row, :, 0:LANES], PART * row), first)
            last = jnp.where(slot == row, turn(field[row, :, LANES : 2 * LANES], PART * row + MARGIN), last)
        left[group] = first
        right[group] = last


def plate_kernel(lab, seg, plate, left, right, label_window):
    tables = seg[...]
    for top in (0, 8):
        for half in range(2):
            labels = lab[top : top + 8, half * LANES : (half + 1) * LANES]
            low = labels & 127
            high = labels >> 7
            value = jnp.zeros((8, LANES), F32)
            for part in range(4):
                table = jnp.broadcast_to(tables[part : part + 1, :], (8, LANES))
                got = jnp.take_along_axis(table, low, axis=1, mode="promise_in_bounds")
                value = jnp.where(high == part, got, value)
            plate[top : top + 8, half * LANES : (half + 1) * LANES] = value
    left[...] = plate[:, 0:LANES]
    right[...] = turn(plate[:, LANES : 2 * LANES], MARGIN)
    part = lax.axis_index("row")
    labels = jnp.where(part >= 4, lab[:, LANES : 2 * LANES], lab[:, 0:LANES])
    label_window[...] = pltpu.roll(labels, (LANES + MARGIN - NARROW - PART * (part % 4)) % LANES, 1)


PIECES = (
    ((0, 0, 0, 80),),
    ((1, 0, 0, 80),),
    ((2, 0, 0, 80),),
    ((3, 0, 0, 80),),
    ((4, 0, 0, 80),),
    ((0, 80, 0, 48), (1, 80, 48, 32)),
    ((1, 112, 0, 16), (2, 80, 16, 48), (3, 80, 64, 16)),
    ((3, 96, 0, 32), (4, 80, 32, 48)),
)


def window_kernel(vel, log, layer, send):
    lane = lanes_of((OWN, LANES))
    turned = {}

    def at(slab, half, amount):
        key = (slab, half, amount % LANES)
        if key not in turned:
            field = (vel, log)[slab // 4]
            turned[key] = turn(field[slab % 4, :, half * LANES : (half + 1) * LANES], amount)
        return turned[key]

    for part in range(8):
        tiles = [None] * 5
        for slab, pieces in enumerate(PIECES):
            for tile, start, first, count in pieces:
                shift = start - first
                amount = MARGIN - PART * part + shift
                edge = LANES + MARGIN - PART * part + shift
                if edge >= start + count:
                    wide = at(slab, 0, amount)
                elif edge <= start:
                    wide = at(slab, 1, amount)
                else:
                    wide = jnp.where(lane < edge, at(slab, 0, amount), at(slab, 1, amount))
                if slab < 4:
                    wide = jnp.where(lane == SPAN - 1, layer[slab], wide)
                if tiles[tile] is None:
                    tiles[tile] = wide
                else:
                    tiles[tile] = jnp.where((lane >= start) & (lane < start + count), wide, tiles[tile])
        for tile in range(5):
            send[part, tile] = tiles[tile]


def inner(edge, own, group, low):
    place = lanes_of((OWN, LANES)) % PART
    near, next_one = (MARGIN - 1, MARGIN - 2) if low else (0, 1)
    if group == 0:
        return jnp.where((place == near) | (place == next_one), 0.0, edge)
    sign = 1 if low else -1
    edge = jnp.where(place == near, turn(own, sign * (MARGIN - 1)), edge)
    return jnp.where(place == next_one, turn(own, sign * (MARGIN - 3)), edge)


def patch_kernel(sent, left, right, from_left, from_right, send):
    lane = lanes_of((OWN, LANES))
    first = lax.axis_index("vert") == 0
    last = lax.axis_index("vert") == lax.axis_size("vert") - 1
    before, after = [], []
    for group in range(2):
        low, high = from_left[group], from_right[group]
        before.append(jnp.where(first, inner(low, left[group], group, True), low))
        after.append(jnp.where(last, inner(high, right[group], group, False), high))
    for part in range(1, 7):
        send[part] = sent[part]
    for part, edges, begin, stop in ((0, before, 0, MARGIN), (7, after, SPAN - MARGIN, SPAN)):
        tiles = [sent[part, tile] for tile in range(5)]
        for slab, pieces in enumerate(PIECES):
            group, row = slab // 4, slab % 4
            end = SPAN - 1 if group == 0 and stop == SPAN else stop
            for tile, start, head, count in pieces:
                low, high = max(begin, head), min(end, head + count)
                if low >= high:
                    continue
                shift = start - head
                moved = turn(edges[group], shift + begin - PART * row)
                tiles[tile] = jnp.where((lane >= low + shift) & (lane < high + shift), moved, tiles[tile])
        for tile in range(5):
            send[part, tile] = tiles[tile]


def rows_kernel(got, plate, left, right, from_left, from_right, up, down, plate_window):
    lane = lanes_of((OWN, LANES))
    first = lax.axis_index("vert") == 0
    last = lax.axis_index("vert") == lax.axis_size("vert") - 1
    before = jnp.where(first, inner(from_left[...], left[...], 1, True), from_left[...])
    after = jnp.where(last, inner(from_right[...], right[...], 1, False), from_right[...])
    part = lax.axis_index("row")
    shift = PART * (part % 4)
    one, two = turn(plate[:, 0:LANES], MARGIN), turn(plate[:, LANES : 2 * LANES], MARGIN)
    head = lane < MARGIN
    tiles = (jnp.where(head, before, one), jnp.where(head, one, two), jnp.where(head, two, turn(after, MARGIN)))
    late = part >= 4
    here = jnp.where(late, tiles[1], tiles[0])
    there = jnp.where(late, tiles[2], tiles[1])
    back = (LANES - shift) % LANES
    window = jnp.where(lane < LANES - shift, pltpu.roll(here, back, 1), pltpu.roll(there, back, 1))
    plate_window[...] = window
    for index in range(TILES + 1):
        values = got[index // 5, index % 5] if index < TILES else window
        at = TILES + 1 + index // 2
        half = 4 * (index % 2)
        up[index] = values[8:16]
        down[index] = values[0:8]
        up[at, half : half + 4, :] = values[4:8]
        down[at, half : half + 4, :] = values[8:12]


def rows_of(index, up, down, total):
    at = total + index // 2
    half = 4 * (index % 2)
    return up[at, half : half + 4, :], up[index], down[index], down[at, half : half + 4, :]


def places(rows=WINDOW):
    step = WINDOW // rows
    row_at = lax.broadcasted_iota(jnp.int32, (rows, LANES), 0)
    lane = lanes_of((rows, LANES))
    across = step * row_at + (lax.axis_index("au") * OWN - HALO)
    along = lane + (lax.axis_index("vert") * (8 * PART) + lax.axis_index("row") * PART - MARGIN)
    across_end = lax.axis_size("au") * OWN
    along_end = lax.axis_size("vert") * 8 * PART
    domain = (across >= 0) & (across < across_end) & (along >= 0) & (along < along_end) & (lane < SPAN)
    return row_at, lane, across, along, across_end, along_end, domain


def middle(ref, at, rows=WINDOW, top=TOP):
    return ref[at, top : top + rows, :]


def four(ref, at):
    centre = middle(ref, at)
    low, high = ref[at, TOP - 1 : TOP - 1 + WINDOW, :], ref[at, TOP + 1 : TOP + 1 + WINDOW, :]
    return low, high, turn(centre, 1), turn(centre, -1)


def slabs(ref, rows=WINDOW, reach=1, top=TOP):
    before, centre = middle(ref, 0, rows, top), middle(ref, 1, rows, top)
    for at in range(ref.shape[0] - 2):
        after = middle(ref, at + 2, rows, top)
        beside = (
            ref[at + 1, top - 1 : top - 1 + rows, :],
            ref[at + 1, top + 1 : top + 1 + rows, :],
            turn(centre, reach),
            turn(centre, -reach),
        )
        yield at, centre, beside, (before, after)
        before, centre = centre, after


def around(ref, rows=WINDOW, reach=1, top=TOP):
    for at, centre, (low, high, left, right), (before, after) in slabs(ref, rows, reach, top):
        yield at, centre, ((low + high) + (left + right)) + (before + after)


def pair_sum(spare, even_lane):
    total = spare[pl.ds(0, HALF, 2), :] + spare[pl.ds(1, HALF, 2), :]
    return total + jnp.where(even_lane, turn(total, -1), turn(total, 1))


def clear_edges(refs, rows=WINDOW, skip=0):
    row = jnp.zeros((1, LANES), F32)
    slab = jnp.zeros((rows, LANES), F32)
    top = TOP + skip
    for ref in refs:
        last = ref.shape[0] - 1
        for at in range(1, last):
            ref[at, top - 1 : top, :] = row
            ref[at, top + rows : top + rows + 1, :] = row
        ref[0, top : top + rows, :] = slab
        ref[last, top : top + rows, :] = slab


def join(ref, rows=WINDOW, skip=0):
    top = TOP + skip
    last = ref.shape[0] - 2
    low = lanes_of((rows, LANES)) < 64
    ref[0, top : top + rows, :] = jnp.where(low, 0.0, turn(middle(ref, last, rows, top), 64))
    ref[last + 1, top : top + rows, :] = jnp.where(low, turn(middle(ref, 1, rows, top), 64), 0.0)


def smooth(out, values, source, factor, rows=WINDOW, reach=1, skip=0):
    top = TOP + skip
    for at, centre, total in around(values, rows, reach, top):
        if source is None:
            result = (1.0 + KEEP) * centre
        else:
            result = KEEP * centre + middle(source, at + 1, rows, top)
        out[at + 1, top : top + rows, :] = result + factor[at, skip : skip + rows, :] * total


def vcycle(f, one, two, zf, za, zb, spare, g, g_top, c, big, cc, kc, ginv, joined):
    even_lane = lanes_of((HALF, LANES)) % 2 == 0
    count = zf.shape[0] - 2

    def close(ref, rows=WINDOW, skip=0):
        if joined:
            join(ref, rows, skip)

    smooth(two, f, None, c)
    close(two)

    first = None
    for at, centre, total in around(two):
        leftover = big[at] * ((middle(f, at + 1) - DAMPING * centre) + c[at] * total)
        if at % 2:
            spare[at // 2] = first + leftover
        first = leftover
    for at in range(count):
        zf[at + 1, TOP : TOP + HALF, :] = kc[at, 0:HALF, :] * pair_sum(spare.at[at], even_lane)
    close(zf, HALF)
    smooth(za, zf, None, cc, HALF, 2)
    close(za, HALF)
    smooth(zb, za, zf, cc, HALF, 2)
    close(zb, HALF)
    smooth(za, zb, zf, cc, 16, 2)
    for at in range(count):
        value = middle(za, at + 1, 16) * ginv[at, 0:16, :]
        spare[at, pl.ds(0, 16, 2), :] = value
        spare[at, pl.ds(1, 16, 2), :] = value
    top = TOP + SKIP
    for at in range(count):
        value = spare[at, SKIP : SKIP + INNER, :]
        for row in (2 * at + 1, 2 * at + 2):
            one[row, top : top + INNER, :] = (
                middle(two, row, INNER, top) + middle(g, row, INNER, g_top + SKIP) * value
            )
    close(one, INNER, SKIP)
    smooth(two, one, f, c, INNER, 1, SKIP)
    close(two, INNER, SKIP)
    smooth(one, two, f, c, INNER, 1, SKIP)


def depth_at(at):
    place = jnp.zeros((8, LANES), jnp.int32) + at
    return jnp.exp(-(LAYERS - 1 - place).astype(F32) / (LAYERS / 4.0))


def tall(values, rows=WINDOW):
    return jnp.concatenate([values] * (rows // 8), axis=0)


def first_kernel(
    got, plate_window, from_low, from_high,
    g, c, big, cc, kc, ginv, vel, x_own, f_own, f_up, f_down,
    packed, f, one, two, zf, za, zb, spare, layer, gc,
):
    domain = places()[-1]
    coarse_domain = places(HALF)[-1]
    clear_edges((f, two, vel, g))
    clear_edges((one,), INNER, SKIP)
    clear_edges((zf, za, zb, gc), HALF)
    for index in range(TILES + 1):
        a, b, d, e = rows_of(index, from_low, from_high, TILES + 1)
        packed[index, 0:4, :] = a
        packed[index, 4:12, :] = b
        packed[index, 12:28, :] = got[index // 5, index % 5] if index < TILES else plate_window[...]
        packed[index, 28:36, :] = d
        packed[index, 36:40, :] = e

    def mirror(pairs):
        speed = lanes_of((1, LANES)) < SPAN
        for index in range(TILES + 1):
            for target, source in pairs:
                value = packed[index, source : source + 1, :]
                if index < TILES and index % 5 < 4:
                    value = jnp.where(speed, 0.0, value)
                packed[index, target : target + 1, :] = value

    @pl.when(lax.axis_index("au") == 0)
    def _():
        mirror(((HALO - 1, HALO), (HALO - 2, HALO + 1)))

    @pl.when(lax.axis_index("au") == lax.axis_size("au") - 1)
    def _():
        mirror(((HALO + OWN, HALO + OWN - 1), (HALO + OWN + 1, HALO + OWN - 2)))

    lane = lanes_of((WINDOW, LANES))
    even_lane = lanes_of((HALF, LANES)) % 2 == 0

    def slab_of(source, slab):
        result = jnp.zeros((WINDOW, LANES), F32)
        for tile, start, first, count in reversed(PIECES[slab]):
            result = jnp.where(lane < first + count, turn(packed[source * 5 + tile], first - start), result)
        return result

    for source in range(8):
        logs = []
        for row in range(4):
            at = source * 4 + row + 1
            speed = slab_of(source, row)
            layer[at] = jnp.broadcast_to(speed[16:24, SPAN - 1 : SPAN], (8, LANES))
            vel[at, TOP : TOP + WINDOW, :] = speed
            logs.append(slab_of(source, 4 + row))
            g[at, TOP : TOP + WINDOW, :] = jnp.exp(0.5 * logs[-1])
        for pair in range(2):
            spare[2 * source + pair] = logs[2 * pair] + logs[2 * pair + 1]
    for at in range(LAYERS // 2):
        gc[at + 1, TOP : TOP + HALF, :] = jnp.exp(0.0625 * pair_sum(spare.at[at], even_lane))
    layer[0] = layer[1]
    layer[LAYERS + 1] = layer[LAYERS]
    g[0] = g[1]
    g[LAYERS + 1] = g[LAYERS]
    gc[0] = gc[1]
    gc[LAYERS // 2 + 1] = gc[LAYERS // 2]

    for at, centre, total in around(gc, HALF, 2):
        per = jnp.where(coarse_domain, DAMPING / total, 0.0)
        for ref, value in ((cc, centre * per), (kc, (0.125 / COARSE_FACTOR) * per), (ginv, 1.0 / centre)):
            ref[at, 0:HALF, :] = value
            ref[at, HALF:HALF_TALL, :] = jnp.zeros((HALF_TALL - HALF, LANES), F32)

    plate = packed[TILES]
    two[1, TOP : TOP + WINDOW, :] = plate
    beside = [plate + other for other in four(two, 1)]
    across_layers = None
    for (at, g_mid, g_four, g_two), (_, v_mid, v_four, v_two) in zip(slabs(g), slabs(vel)):
        depth = depth_at(at)
        level = layer[at + 1]
        depth_tall, twice = tall(depth), tall(2.0 * level)
        total_g = (g_four[0] + g_four[1]) + (g_four[2] + g_four[3])
        total_g = total_g + (g_two[0] + g_two[1])
        total = jnp.zeros((WINDOW, LANES), F32)
        for g_n, v_n, s_n in zip(g_four, v_four, beside):
            total = total + g_n * (depth_tall * s_n + twice) * (v_mid - v_n)
        total = g_mid * total
        for other, g_n, v_n in zip((at, at + 2), g_two, v_two):
            place = min(max(other - 1, 0), LAYERS - 1)
            if other == at and at > 0:
                total = total - across_layers
                continue
            scale = tall(depth + depth_at(place)) * plate + tall(level + layer[other])
            across_layers = (g_mid * g_n) * scale * (v_mid - v_n)
            total = total + across_layers
        per = jnp.where(domain, DAMPING / total_g, 0.0)
        c[at] = g_mid * per
        big[at] = total_g * (1.0 / DAMPING)
        f[at + 1, TOP : TOP + WINDOW, :] = -0.5 * total * per
    vcycle(f, one, two, zf, za, zb, spare, g, TOP, c, big, cc, kc, ginv, False)

    own_lane = lanes_of((OWN, LANES))
    sent = []
    for at in range(LAYERS):
        ratio = 1.0 / g[at + 1, TOP + HALO : TOP + HALO + OWN, :]
        x = one[at + 1, TOP + HALO : TOP + HALO + OWN, :] * ratio
        x_own[at] = x
        sent.append(-(x * (c[at, HALO : HALO + OWN, :] * ratio)))
    for index in range(16):
        both = jnp.where(own_lane < 64, turn(sent[index], -NARROW), turn(sent[index + 16], 64 - NARROW))
        start = 4 * (index % 2)
        f_own[index] = both
        f_up[index] = both[8:16]
        f_down[index] = both[0:8]
        f_up[16 + index // 2, start : start + 4, :] = both[4:8]
        f_down[16 + index // 2, start : start + 4, :] = both[8:12]


def side_kernel(
    g, c, big, cc, kc, ginv, vel, x_own, label_window,
    inc, ones, g_two, c_two, big_two, cc_two, kc_two, ginv_two, vel_two,
):
    slot = lanes_of((OWN, LANES)) // PART
    for part in range(8):
        tile = turn(x_own[4 * part], -MARGIN)
        for row in range(1, 4):
            tile = jnp.where(slot == row, turn(x_own[4 * part + row], PART * row - MARGIN), tile)
        inc[part] = tile
    low = label_window[...] & 127
    place = lax.broadcasted_iota(jnp.int32, (LANES, LANES), 0)
    for at in range(OWN):
        hit = jnp.where(low[at : at + 1, :] == place, 1.0, 0.0)
        ones[:, at * LANES : (at + 1) * LANES] = hit.astype(jnp.bfloat16)
    for source, target in ((g, g_two), (vel, vel_two), (c, c_two), (big, big_two), (cc, cc_two), (kc, kc_two), (ginv, ginv_two)):
        rows = target.shape[1]
        top = TOP if source.shape[1] == PAD_ROWS else 0
        first = lanes_of((rows, LANES)) < 64
        for at in range(target.shape[0]):
            upper = at + (8 if rows == HALF_TALL else 16)
            target[at] = jnp.where(
                first, turn(middle(source, at, rows, top), -NARROW), turn(middle(source, upper, rows, top), 64 - NARROW)
            )


def second_kernel(
    g, c, big, cc, kc, ginv, vel, f_own, from_low, from_high, inc, label_window, ones,
    send,
    f, one, two, zf, za, zb, spare, layers,
):
    count = LAYERS // 2
    clear_edges((f, two))
    clear_edges((one,), INNER, SKIP)
    clear_edges((zf, za, zb), HALF)
    for index in range(count):
        start = 4 * (index % 2)
        at = index + 1
        f[at, TOP : TOP + 4, :] = from_low[16 + index // 2, start : start + 4, :]
        f[at, TOP + 4 : TOP + 12, :] = from_low[index]
        f[at, TOP + HALO : TOP + HALO + OWN, :] = f_own[index]
        f[at, TOP + 28 : TOP + 36, :] = from_high[index]
        f[at, TOP + 36 : TOP + 40, :] = from_high[16 + index // 2, start : start + 4, :]
    join(f)
    vcycle(f, one, two, zf, za, zb, spare, g, 0, c, big, cc, kc, ginv, True)

    top = TOP + SKIP
    for at in range(count):
        two[at + 1, top : top + INNER, :] = middle(one, at + 1, INNER, top) / middle(g, at + 1, INNER, SKIP)
    join(two, INNER, SKIP)
    row_at = SKIP + lax.broadcasted_iota(jnp.int32, (INNER, LANES), 0)
    lane = lanes_of((INNER, LANES))
    low = lane < 64
    place = lane % 64 + NARROW
    across = row_at + (lax.axis_index("au") * OWN - HALO)
    along = place + (lax.axis_index("vert") * (8 * PART) + lax.axis_index("row") * PART - MARGIN)
    own = (row_at >= HALO) & (row_at < HALO + OWN) & (place >= MARGIN) & (place < MARGIN + PART)
    shares = [
        jnp.where(edge, 1.0, 0.5)
        for edge in (
            across == 0,
            across == lax.axis_size("au") * OWN - 1,
            along == 0,
            along == lax.axis_size("vert") * 8 * PART - 1,
        )
    ]
    column = jnp.zeros((INNER, LANES), F32)
    upper = (lanes_of((8, LANES)) >= 64).astype(jnp.int32) * count
    walk = zip(slabs(g, INNER, 1, SKIP), slabs(vel, INNER, 1, SKIP), slabs(two, INNER, 1, top))
    for (at, g_mid, g_four, g_two), (_, v_mid, v_four, v_two), (_, x_mid, x_four, x_two) in walk:
        total = jnp.zeros((INNER, LANES), F32)
        for share, g_n, v_n, x_n in zip(shares, g_four, v_four, x_four):
            total = total + (share * g_n) * ((x_n - x_mid) * (v_n - v_mid))
        for other, g_n, v_n, x_n in zip((at, at + 2), g_two, v_two, x_two):
            share = 0.5
            if other == 0:
                share = jnp.where(low, 1.0, 0.5)
            if other == count + 1:
                share = jnp.where(low, 0.5, 1.0)
            total = total + (share * g_n) * ((x_n - x_mid) * (v_n - v_mid))
        total = jnp.where(own, g_mid * total, 0.0)
        column = column + tall(depth_at(upper + at), INNER) * total
        layers[at] = jnp.sum(total.reshape(INNER // 8, 8, LANES), axis=0)
    level = jnp.sum(layers[...], axis=1)

    high = label_window[...] >> 7
    column = jnp.where(low, column + turn(column, 64), 0.0)
    sums = column[HALO - SKIP : HALO - SKIP + OWN, :]
    kind = lax.broadcasted_iota(jnp.int32, (4, LANES), 0)
    left = []
    for at in range(OWN):
        value = jnp.where(high[at : at + 1, :] == kind, sums[at : at + 1, :], 0.0)
        first = value.astype(jnp.bfloat16).astype(F32)
        rest = value - first
        then = rest.astype(jnp.bfloat16).astype(F32)
        left.append(jnp.concatenate([first, then, rest - then, jnp.zeros_like(first)], axis=0).astype(jnp.bfloat16))
    product = lax.dot_general(
        jnp.concatenate(left, axis=1), ones[...], (((1,), (1,)), ((), ())), preferred_element_type=F32
    )
    segments = (product[0:4] + product[4:8]) + product[8:12]

    slot = lanes_of((OWN, LANES)) // PART
    lower = lanes_of((4, LANES)) < 64
    for part in range(8):
        half, at = part // 4, 4 * (part % 4)
        tile = None
        for row in range(4):
            x = two[at + row + 1, TOP + HALO : TOP + HALO + OWN, :]
            x = turn(x, PART * row - (MARGIN - NARROW) - 64 * half)
            tile = x if tile is None else jnp.where(slot == row, x, tile)
        send[part, 0:16, :] = inc[part]
        send[part, 16:32, :] = tile
        here = level[at : at + 4, :]
        here = jnp.where(lower, 0.0, here) if half else jnp.where(lower, here, 0.0)
        send[part, 32:40, :] = jnp.concatenate([segments, here], axis=0)


def sum_kernel(got, spread):
    total = got[0, 32:40, :]
    for source in range(1, 8):
        total = total + got[source, 32:40, :]
    level = jnp.zeros((1, LANES), F32)
    lane = lanes_of((1, LANES))
    for row in range(4):
        level = jnp.where(lane == row, jnp.sum(total[4 + row : 5 + row, :], axis=1, keepdims=True), level)
    pieces = [total[row : row + 1, :] for row in range(4)] + [level]
    line = jnp.concatenate(pieces, axis=1)
    for other in range(spread.shape[0]):
        spread[other] = line


def place_kernel(got, parts, inc, adj, segments, layers):
    lane = lanes_of((OWN, LANES))
    slot = lane // PART
    for out, start in ((inc, 0), (adj, 16)):
        for row in range(4):
            for half in range(2):
                tile = jnp.zeros((OWN, LANES), F32)
                for source in range(4):
                    piece = got[4 * half + source, start : start + 16, :]
                    tile = jnp.where(slot == source, turn(piece, PART * (source - row)), tile)
                out[row, :, half * LANES : (half + 1) * LANES] = tile
    cells = LAYERS * lax.axis_size("au") * OWN * lax.axis_size("vert") * 8 * PART
    total = jnp.sum(parts[...], axis=0)
    lines = [total[:, row * LANES : (row + 1) * LANES] for row in range(4)]
    segments[...] = jnp.concatenate(lines, axis=0) * (1.0 / (cells / NSEG) ** 0.5)
    layers[...] = total[:, 4 * LANES : 4 * LANES + 4] * (1.0 / (cells / LAYERS) ** 0.5)


def shards(velocity, log_visc, labels, seg_dir, layer_dir):
    vert = lax.axis_size("vert")
    across = lax.axis_size("au")
    ahead = [(i, (i + 1) % vert) for i in range(vert)]
    back = [((i + 1) % vert, i) for i in range(vert)]
    upward = [(i, i + 1) for i in range(across - 1)]
    downward = [(i + 1, i) for i in range(across - 1)]
    vmem = pl.BlockSpec(memory_space=pltpu.VMEM)
    hbm = pl.BlockSpec(memory_space=pltpu.HBM)
    label_tile = jax.ShapeDtypeStruct((OWN, LANES), jnp.int32)
    tile, pair, field = sds(OWN, LANES), sds(2, OWN, LANES), sds(4, OWN, 2 * LANES)

    left, right, vel, log = call(
        edge_kernel,
        (pair, pair, field, field),
        [pltpu.SemaphoreType.DMA((2,))],
        in_specs=[hbm] * 2,
        limit=EDGE_LIMIT,
    )(velocity, log_visc)
    from_left = lax.ppermute(right, "vert", ahead)
    from_right = lax.ppermute(left, "vert", back)
    plate, plate_left, plate_right, label_window = call(
        plate_kernel, (sds(OWN, 2 * LANES), tile, tile, label_tile)
    )(labels, seg_dir.reshape(4, LANES))
    plate_before = lax.ppermute(plate_right, "vert", ahead)
    plate_after = lax.ppermute(plate_left, "vert", back)
    send = call(
        window_kernel,
        sds(8, 5, OWN, LANES),
        in_specs=[vmem, vmem, pl.BlockSpec(memory_space=pltpu.SMEM)],
    )(vel, log, layer_dir)
    send = call(patch_kernel, sds(8, 5, OWN, LANES))(send, left, right, from_left, from_right)
    got = lax.all_to_all(send, "row", 0, 0, tiled=True)
    up, down, plate_window = call(rows_kernel, (sds(62, 8, LANES), sds(62, 8, LANES), tile))(
        got, plate, plate_left, plate_right, plate_before, plate_after
    )
    from_low = lax.ppermute(up, "au", upward)
    from_high = lax.ppermute(down, "au", downward)
    fine = sds(LAYERS, WINDOW, LANES)
    fine_padded = sds(LAYERS + 2, PAD_ROWS, LANES)
    coarse = sds(LAYERS // 2, HALF_TALL, LANES)

    def scratch(layers):
        return (
            [pltpu.VMEM((layers + 2, PAD_ROWS, LANES), F32)] * 3
            + [pltpu.VMEM((layers // 2 + 2, HALF_ROWS, LANES), F32)] * 3
            + [pltpu.VMEM((layers // 2 + 1, WINDOW, LANES), F32)]
        )

    *factors, x_own, f_own, f_up, f_down = call(
        first_kernel,
        (fine_padded, fine, fine, coarse, coarse, coarse, fine_padded)
        + (sds(LAYERS, OWN, LANES), sds(LAYERS // 2, OWN, LANES), sds(25, 8, LANES), sds(25, 8, LANES)),
        [pltpu.VMEM((TILES + 2, WINDOW, LANES), F32)]
        + scratch(LAYERS)
        + [pltpu.VMEM((LAYERS + 2, 8, LANES), F32), pltpu.VMEM((LAYERS // 2 + 2, HALF_ROWS, LANES), F32)],
    )(got, plate_window, from_low, from_high)
    from_low = lax.ppermute(f_up, "au", upward)
    from_high = lax.ppermute(f_down, "au", downward)
    fine = sds(LAYERS // 2, WINDOW, LANES)
    fine_closed = sds(LAYERS // 2 + 2, WINDOW, LANES)
    coarse = sds(LAYERS // 4, HALF_TALL, LANES)
    inc, ones, *factors = call(
        side_kernel,
        (sds(8, OWN, LANES), jax.ShapeDtypeStruct((LANES, OWN * LANES), jnp.bfloat16))
        + (fine_closed, fine, fine, coarse, coarse, coarse, fine_closed),
    )(*factors, x_own, label_window)
    send = call(second_kernel, sds(8, 40, LANES), scratch(LAYERS // 2) + [pltpu.VMEM((LAYERS // 2, 8, LANES), F32)])(
        *factors, f_own, from_low, from_high, inc, label_window, ones
    )
    got = lax.all_to_all(send, "row", 0, 0, tiled=True)
    spread = call(sum_kernel, sds(across * vert, 1, 5 * LANES))(got)
    parts = lax.all_to_all(spread, ("au", "vert"), 0, 0, tiled=True)
    increment, adjoint, hv_segments, hv_layers = call(place_kernel, (field, field, sds(4, LANES), sds(1, 4)))(
        got, parts
    )
    return increment, adjoint, hv_segments.reshape(NSEG), hv_layers.reshape(4)


def solution(mesh):
    in_specs = (P("row", "au", "vert"), P("row", "au", "vert"), P("au", "vert"), P(), P("row"))
    out_specs = (P("row", "au", "vert"), P("row", "au", "vert"), P(), P("row"))
    return jax.shard_map(shards, mesh=mesh, in_specs=in_specs, out_specs=out_specs, check_vma=False)
```

```python
import jax
import jax.numpy as jnp
from jax import lax
from jax.experimental import pallas as pl
from jax.experimental.pallas import tpu as pltpu
from jax.sharding import PartitionSpec as P

NSEG = 512
DAMPING = 0.7
KEEP = 1.0 - DAMPING
COARSE_FACTOR = 0.25

LAYERS = 32
OWN = 16
HALO = 12
WINDOW = OWN + 2 * HALO
PART = 32
MARGIN = 24
SPAN = PART + 2 * MARGIN
LANES = 128
TOP = 8
HALF = WINDOW // 2
HALF_ROWS = 40
HALF_TALL = 24
INNER = 24
SKIP = 8
NARROW = 8
PAD_ROWS = WINDOW + 2 * TOP
TILES = 40
F32 = jnp.float32
VMEM_LIMIT = 24 * 1024 * 1024
EDGE_LIMIT = 56360000


def lanes_of(shape):
    return lax.broadcasted_iota(jnp.int32, shape, len(shape) - 1)


def turn(values, amount):
    return pltpu.roll(values, amount % LANES, values.ndim - 1)


def call(kernel, outs, scratch=(), limit=VMEM_LIMIT, **more):
    return pl.pallas_call(
        kernel,
        out_shape=outs,
        **more,
        scratch_shapes=list(scratch),
        compiler_params=pltpu.CompilerParams(vmem_limit_bytes=limit),
    )


def sds(*shape):
    return jax.ShapeDtypeStruct(shape, F32)


def edge_kernel(vel_in, log_in, left, right, vel, log, sems):
    copies = [
        pltpu.make_async_copy(source, target, sems.at[number])
        for number, (source, target) in enumerate(((vel_in, vel), (log_in, log)))
    ]
    for copy in copies:
        copy.start()
    for copy in copies:
        copy.wait()
    slot = lanes_of((OWN, LANES)) // PART
    for group, field in enumerate((vel, log)):
        first = field[0, :, 0:LANES]
        last = turn(field[0, :, LANES : 2 * LANES], MARGIN)
        for row in range(1, 4):
            first = jnp.where(slot == row, turn(field[row, :, 0:LANES], PART * row), first)
            last = jnp.where(slot == row, turn(field[row, :, LANES : 2 * LANES], PART * row + MARGIN), last)
        left[group] = first
        right[group] = last


def plate_kernel(lab, seg, plate, left, right, label_window):
    tables = seg[...]
    for top in (0, 8):
        for half in range(2):
            labels = lab[top : top + 8, half * LANES : (half + 1) * LANES]
            low = labels & 127
            high = labels >> 7
            value = jnp.zeros((8, LANES), F32)
            for part in range(4):
                table = jnp.broadcast_to(tables[part : part + 1, :], (8, LANES))
                got = jnp.take_along_axis(table, low, axis=1, mode="promise_in_bounds")
                value = jnp.where(high == part, got, value)
            plate[top : top + 8, half * LANES : (half + 1) * LANES] = value
    left[...] = plate[:, 0:LANES]
    right[...] = turn(plate[:, LANES : 2 * LANES], MARGIN)
    part = lax.axis_index("row")
    labels = jnp.where(part >= 4, lab[:, LANES : 2 * LANES], lab[:, 0:LANES])
    label_window[...] = pltpu.roll(labels, (LANES + MARGIN - NARROW - PART * (part % 4)) % LANES, 1)


PIECES = (
    ((0, 0, 0, 80),),
    ((1, 0, 0, 80),),
    ((2, 0, 0, 80),),
    ((3, 0, 0, 80),),
    ((4, 0, 0, 80),),
    ((0, 80, 0, 48), (1, 80, 48, 32)),
    ((1, 112, 0, 16), (2, 80, 16, 48), (3, 80, 64, 16)),
    ((3, 96, 0, 32), (4, 80, 32, 48)),
)


def window_kernel(vel, log, layer, send):
    lane = lanes_of((OWN, LANES))
    turned = {}

    def at(slab, half, amount):
        key = (slab, half, amount % LANES)
        if key not in turned:
            field = (vel, log)[slab // 4]
            turned[key] = turn(field[slab % 4, :, half * LANES : (half + 1) * LANES], amount)
        return turned[key]

    for part in range(8):
        tiles = [None] * 5
        for slab, pieces in enumerate(PIECES):
            for tile, start, first, count in pieces:
                shift = start - first
                amount = MARGIN - PART * part + shift
                edge = LANES + MARGIN - PART * part + shift
                if edge >= start + count:
                    wide = at(slab, 0, amount)
                elif edge <= start:
                    wide = at(slab, 1, amount)
                else:
                    wide = jnp.where(lane < edge, at(slab, 0, amount), at(slab, 1, amount))
                if slab < 4:
                    wide = jnp.where(lane == SPAN - 1, layer[slab], wide)
                if tiles[tile] is None:
                    tiles[tile] = wide
                else:
                    tiles[tile] = jnp.where((lane >= start) & (lane < start + count), wide, tiles[tile])
        for tile in range(5):
            send[part, tile] = tiles[tile]


def inner(edge, own, group, low):
    place = lanes_of((OWN, LANES)) % PART
    near, next_one = (MARGIN - 1, MARGIN - 2) if low else (0, 1)
    if group == 0:
        return jnp.where((place == near) | (place == next_one), 0.0, edge)
    sign = 1 if low else -1
    edge = jnp.where(place == near, turn(own, sign * (MARGIN - 1)), edge)
    return jnp.where(place == next_one, turn(own, sign * (MARGIN - 3)), edge)


def patch_kernel(sent, left, right, from_left, from_right, send):
    lane = lanes_of((OWN, LANES))
    first = lax.axis_index("vert") == 0
    last = lax.axis_index("vert") == lax.axis_size("vert") - 1
    before, after = [], []
    for group in range(2):
        low, high = from_left[group], from_right[group]
        before.append(jnp.where(first, inner(low, left[group], group, True), low))
        after.append(jnp.where(last, inner(high, right[group], group, False), high))
    for part in range(1, 7):
        send[part] = sent[part]
    for part, edges, begin, stop in ((0, before, 0, MARGIN), (7, after, SPAN - MARGIN, SPAN)):
        tiles = [sent[part, tile] for tile in range(5)]
        for slab, pieces in enumerate(PIECES):
            group, row = slab // 4, slab % 4
            end = SPAN - 1 if group == 0 and stop == SPAN else stop
            for tile, start, head, count in pieces:
                low, high = max(begin, head), min(end, head + count)
                if low >= high:
                    continue
                shift = start - head
                moved = turn(edges[group], shift + begin - PART * row)
                tiles[tile] = jnp.where((lane >= low + shift) & (lane < high + shift), moved, tiles[tile])
        for tile in range(5):
            send[part, tile] = tiles[tile]


def plate_window_kernel(plate, left, right, from_left, from_right, plate_window):
    lane = lanes_of((OWN, LANES))
    first = lax.axis_index("vert") == 0
    last = lax.axis_index("vert") == lax.axis_size("vert") - 1
    before = jnp.where(first, inner(from_left[...], left[...], 1, True), from_left[...])
    after = jnp.where(last, inner(from_right[...], right[...], 1, False), from_right[...])
    part = lax.axis_index("row")
    shift = PART * (part % 4)
    one, two = turn(plate[:, 0:LANES], MARGIN), turn(plate[:, LANES : 2 * LANES], MARGIN)
    head = lane < MARGIN
    tiles = (jnp.where(head, before, one), jnp.where(head, one, two), jnp.where(head, two, turn(after, MARGIN)))
    late = part >= 4
    here = jnp.where(late, tiles[1], tiles[0])
    there = jnp.where(late, tiles[2], tiles[1])
    back = (LANES - shift) % LANES
    plate_window[...] = jnp.where(lane < LANES - shift, pltpu.roll(here, back, 1), pltpu.roll(there, back, 1))


def rows_kernel(got, plate_window, up, down):
    window = plate_window[...]
    for index in range(TILES + 1):
        values = got[index // 5, index % 5] if index < TILES else window
        at = TILES + 1 + index // 2
        half = 4 * (index % 2)
        up[index] = values[8:16]
        down[index] = values[0:8]
        up[at, half : half + 4, :] = values[4:8]
        down[at, half : half + 4, :] = values[8:12]


def rows_of(index, up, down, total):
    at = total + index // 2
    half = 4 * (index % 2)
    return up[at, half : half + 4, :], up[index], down[index], down[at, half : half + 4, :]


def places(rows=WINDOW):
    step = WINDOW // rows
    row_at = lax.broadcasted_iota(jnp.int32, (rows, LANES), 0)
    lane = lanes_of((rows, LANES))
    across = step * row_at + (lax.axis_index("au") * OWN - HALO)
    along = lane + (lax.axis_index("vert") * (8 * PART) + lax.axis_index("row") * PART - MARGIN)
    across_end = lax.axis_size("au") * OWN
    along_end = lax.axis_size("vert") * 8 * PART
    domain = (across >= 0) & (across < across_end) & (along >= 0) & (along < along_end) & (lane < SPAN)
    return row_at, lane, across, along, across_end, along_end, domain


def middle(ref, at, rows=WINDOW, top=TOP):
    return ref[at, top : top + rows, :]


def four(ref, at):
    centre = middle(ref, at)
    low, high = ref[at, TOP - 1 : TOP - 1 + WINDOW, :], ref[at, TOP + 1 : TOP + 1 + WINDOW, :]
    return low, high, turn(centre, 1), turn(centre, -1)


def slabs(ref, rows=WINDOW, reach=1, top=TOP):
    before, centre = middle(ref, 0, rows, top), middle(ref, 1, rows, top)
    for at in range(ref.shape[0] - 2):
        after = middle(ref, at + 2, rows, top)
        beside = (
            ref[at + 1, top - 1 : top - 1 + rows, :],
            ref[at + 1, top + 1 : top + 1 + rows, :],
            turn(centre, reach),
            turn(centre, -reach),
        )
        yield at, centre, beside, (before, after)
        before, centre = centre, after


def around(ref, rows=WINDOW, reach=1, top=TOP):
    for at, centre, (low, high, left, right), (before, after) in slabs(ref, rows, reach, top):
        yield at, centre, ((low + high) + (left + right)) + (before + after)


def pair_sum(spare, even_lane):
    total = spare[pl.ds(0, HALF, 2), :] + spare[pl.ds(1, HALF, 2), :]
    return total + jnp.where(even_lane, turn(total, -1), turn(total, 1))


def clear_edges(refs, rows=WINDOW, skip=0):
    row = jnp.zeros((1, LANES), F32)
    slab = jnp.zeros((rows, LANES), F32)
    top = TOP + skip
    for ref in refs:
        last = ref.shape[0] - 1
        for at in range(1, last):
            ref[at, top - 1 : top, :] = row
            ref[at, top + rows : top + rows + 1, :] = row
        ref[0, top : top + rows, :] = slab
        ref[last, top : top + rows, :] = slab


def join(ref, rows=WINDOW, skip=0):
    top = TOP + skip
    last = ref.shape[0] - 2
    low = lanes_of((rows, LANES)) < 64
    ref[0, top : top + rows, :] = jnp.where(low, 0.0, turn(middle(ref, last, rows, top), 64))
    ref[last + 1, top : top + rows, :] = jnp.where(low, turn(middle(ref, 1, rows, top), 64), 0.0)


def smooth(out, values, source, factor, rows=WINDOW, reach=1, skip=0):
    top = TOP + skip
    for at, centre, total in around(values, rows, reach, top):
        if source is None:
            result = (1.0 + KEEP) * centre
        else:
            result = KEEP * centre + middle(source, at + 1, rows, top)
        out[at + 1, top : top + rows, :] = result + factor[at, skip : skip + rows, :] * total


def vcycle(f, one, two, zf, za, zb, spare, g, g_top, c, big, cc, kc, ginv, joined):
    even_lane = lanes_of((HALF, LANES)) % 2 == 0
    count = zf.shape[0] - 2

    def close(ref, rows=WINDOW, skip=0):
        if joined:
            join(ref, rows, skip)

    smooth(two, f, None, c)
    close(two)

    first = None
    for at, centre, total in around(two):
        leftover = big[at] * ((middle(f, at + 1) - DAMPING * centre) + c[at] * total)
        if at % 2:
            spare[at // 2] = first + leftover
        first = leftover
    for at in range(count):
        zf[at + 1, TOP : TOP + HALF, :] = kc[at, 0:HALF, :] * pair_sum(spare.at[at], even_lane)
    close(zf, HALF)
    smooth(za, zf, None, cc, HALF, 2)
    close(za, HALF)
    smooth(zb, za, zf, cc, HALF, 2)
    close(zb, HALF)
    smooth(za, zb, zf, cc, 16, 2)
    for at in range(count):
        value = middle(za, at + 1, 16) * ginv[at, 0:16, :]
        spare[at, pl.ds(0, 16, 2), :] = value
        spare[at, pl.ds(1, 16, 2), :] = value
    top = TOP + SKIP
    for at in range(count):
        value = spare[at, SKIP : SKIP + INNER, :]
        for row in (2 * at + 1, 2 * at + 2):
            one[row, top : top + INNER, :] = (
                middle(two, row, INNER, top) + middle(g, row, INNER, g_top + SKIP) * value
            )
    close(one, INNER, SKIP)
    smooth(two, one, f, c, INNER, 1, SKIP)
    close(two, INNER, SKIP)
    smooth(one, two, f, c, INNER, 1, SKIP)


def depth_at(at):
    place = jnp.zeros((8, LANES), jnp.int32) + at
    return jnp.exp(-(LAYERS - 1 - place).astype(F32) / (LAYERS / 4.0))


def tall(values, rows=WINDOW):
    return jnp.concatenate([values] * (rows // 8), axis=0)


def first_kernel(
    got, plate_window, from_low, from_high,
    g, c, big, cc, kc, ginv, vel, x_own, f_own, f_up, f_down,
    packed, f, one, two, zf, za, zb, spare, layer, gc,
):
    domain = places()[-1]
    coarse_domain = places(HALF)[-1]
    clear_edges((f, two, vel, g))
    clear_edges((one,), INNER, SKIP)
    clear_edges((zf, za, zb, gc), HALF)
    for index in range(TILES + 1):
        a, b, d, e = rows_of(index, from_low, from_high, TILES + 1)
        packed[index, 0:4, :] = a
        packed[index, 4:12, :] = b
        packed[index, 12:28, :] = got[index // 5, index % 5] if index < TILES else plate_window[...]
        packed[index, 28:36, :] = d
        packed[index, 36:40, :] = e

    def mirror(pairs):
        speed = lanes_of((1, LANES)) < SPAN
        for index in range(TILES + 1):
            for target, source in pairs:
                value = packed[index, source : source + 1, :]
                if index < TILES and index % 5 < 4:
                    value = jnp.where(speed, 0.0, value)
                packed[index, target : target + 1, :] = value

    @pl.when(lax.axis_index("au") == 0)
    def _():
        mirror(((HALO - 1, HALO), (HALO - 2, HALO + 1)))

    @pl.when(lax.axis_index("au") == lax.axis_size("au") - 1)
    def _():
        mirror(((HALO + OWN, HALO + OWN - 1), (HALO + OWN + 1, HALO + OWN - 2)))

    lane = lanes_of((WINDOW, LANES))
    even_lane = lanes_of((HALF, LANES)) % 2 == 0

    def slab_of(source, slab):
        result = jnp.zeros((WINDOW, LANES), F32)
        for tile, start, first, count in reversed(PIECES[slab]):
            result = jnp.where(lane < first + count, turn(packed[source * 5 + tile], first - start), result)
        return result

    for source in range(8):
        logs = []
        for row in range(4):
            at = source * 4 + row + 1
            speed = slab_of(source, row)
            layer[at] = jnp.broadcast_to(speed[16:24, SPAN - 1 : SPAN], (8, LANES))
            vel[at, TOP : TOP + WINDOW, :] = speed
            logs.append(slab_of(source, 4 + row))
            g[at, TOP : TOP + WINDOW, :] = jnp.exp(0.5 * logs[-1])
        for pair in range(2):
            spare[2 * source + pair] = logs[2 * pair] + logs[2 * pair + 1]
    for at in range(LAYERS // 2):
        gc[at + 1, TOP : TOP + HALF, :] = jnp.exp(0.0625 * pair_sum(spare.at[at], even_lane))
    layer[0] = layer[1]
    layer[LAYERS + 1] = layer[LAYERS]
    g[0] = g[1]
    g[LAYERS + 1] = g[LAYERS]
    gc[0] = gc[1]
    gc[LAYERS // 2 + 1] = gc[LAYERS // 2]

    for at, centre, total in around(gc, HALF, 2):
        per = jnp.where(coarse_domain, DAMPING / total, 0.0)
        for ref, value in ((cc, centre * per), (kc, (0.125 / COARSE_FACTOR) * per), (ginv, 1.0 / centre)):
            ref[at, 0:HALF, :] = value
            ref[at, HALF:HALF_TALL, :] = jnp.zeros((HALF_TALL - HALF, LANES), F32)

    plate = packed[TILES]
    two[1, TOP : TOP + WINDOW, :] = plate
    beside = [plate + other for other in four(two, 1)]
    across_layers = None
    for (at, g_mid, g_four, g_two), (_, v_mid, v_four, v_two) in zip(slabs(g), slabs(vel)):
        depth = depth_at(at)
        level = layer[at + 1]
        depth_tall, twice = tall(depth), tall(2.0 * level)
        total_g = (g_four[0] + g_four[1]) + (g_four[2] + g_four[3])
        total_g = total_g + (g_two[0] + g_two[1])
        total = jnp.zeros((WINDOW, LANES), F32)
        for g_n, v_n, s_n in zip(g_four, v_four, beside):
            total = total + g_n * (depth_tall * s_n + twice) * (v_mid - v_n)
        total = g_mid * total
        for other, g_n, v_n in zip((at, at + 2), g_two, v_two):
            place = min(max(other - 1, 0), LAYERS - 1)
            if other == at and at > 0:
                total = total - across_layers
                continue
            scale = tall(depth + depth_at(place)) * plate + tall(level + layer[other])
            across_layers = (g_mid * g_n) * scale * (v_mid - v_n)
            total = total + across_layers
        per = jnp.where(domain, DAMPING / total_g, 0.0)
        c[at] = g_mid * per
        big[at] = total_g * (1.0 / DAMPING)
        f[at + 1, TOP : TOP + WINDOW, :] = -0.5 * total * per
    vcycle(f, one, two, zf, za, zb, spare, g, TOP, c, big, cc, kc, ginv, False)

    own_lane = lanes_of((OWN, LANES))
    sent = []
    for at in range(LAYERS):
        ratio = 1.0 / g[at + 1, TOP + HALO : TOP + HALO + OWN, :]
        x = one[at + 1, TOP + HALO : TOP + HALO + OWN, :] * ratio
        x_own[at] = x
        sent.append(-(x * (c[at, HALO : HALO + OWN, :] * ratio)))
    for index in range(16):
        both = jnp.where(own_lane < 64, turn(sent[index], -NARROW), turn(sent[index + 16], 64 - NARROW))
        start = 4 * (index % 2)
        f_own[index] = both
        f_up[index] = both[8:16]
        f_down[index] = both[0:8]
        f_up[16 + index // 2, start : start + 4, :] = both[4:8]
        f_down[16 + index // 2, start : start + 4, :] = both[8:12]


def side_kernel(
    g, c, big, cc, kc, ginv, vel, x_own, label_window,
    inc, ones, g_two, c_two, big_two, cc_two, kc_two, ginv_two, vel_two,
):
    slot = lanes_of((OWN, LANES)) // PART
    for part in range(8):
        tile = turn(x_own[4 * part], -MARGIN)
        for row in range(1, 4):
            tile = jnp.where(slot == row, turn(x_own[4 * part + row], PART * row - MARGIN), tile)
        inc[part] = tile
    low = label_window[...] & 127
    place = lax.broadcasted_iota(jnp.int32, (LANES, LANES), 0)
    for at in range(OWN):
        hit = jnp.where(low[at : at + 1, :] == place, 1.0, 0.0)
        ones[:, at * LANES : (at + 1) * LANES] = hit.astype(jnp.bfloat16)
    for source, target in ((g, g_two), (vel, vel_two), (c, c_two), (big, big_two), (cc, cc_two), (kc, kc_two), (ginv, ginv_two)):
        rows = target.shape[1]
        top = TOP if source.shape[1] == PAD_ROWS else 0
        first = lanes_of((rows, LANES)) < 64
        for at in range(target.shape[0]):
            upper = at + (8 if rows == HALF_TALL else 16)
            target[at] = jnp.where(
                first, turn(middle(source, at, rows, top), -NARROW), turn(middle(source, upper, rows, top), 64 - NARROW)
            )


def second_kernel(
    g, c, big, cc, kc, ginv, vel, f_own, from_low, from_high, inc, label_window, ones,
    send,
    f, one, two, zf, za, zb, spare, layers,
):
    count = LAYERS // 2
    clear_edges((f, two))
    clear_edges((one,), INNER, SKIP)
    clear_edges((zf, za, zb), HALF)
    for index in range(count):
        start = 4 * (index % 2)
        at = index + 1
        f[at, TOP : TOP + 4, :] = from_low[16 + index // 2, start : start + 4, :]
        f[at, TOP + 4 : TOP + 12, :] = from_low[index]
        f[at, TOP + HALO : TOP + HALO + OWN, :] = f_own[index]
        f[at, TOP + 28 : TOP + 36, :] = from_high[index]
        f[at, TOP + 36 : TOP + 40, :] = from_high[16 + index // 2, start : start + 4, :]
    join(f)
    vcycle(f, one, two, zf, za, zb, spare, g, 0, c, big, cc, kc, ginv, True)

    top = TOP + SKIP
    for at in range(count):
        two[at + 1, top : top + INNER, :] = middle(one, at + 1, INNER, top) / middle(g, at + 1, INNER, SKIP)
    join(two, INNER, SKIP)
    row_at = SKIP + lax.broadcasted_iota(jnp.int32, (INNER, LANES), 0)
    lane = lanes_of((INNER, LANES))
    low = lane < 64
    place = lane % 64 + NARROW
    across = row_at + (lax.axis_index("au") * OWN - HALO)
    along = place + (lax.axis_index("vert") * (8 * PART) + lax.axis_index("row") * PART - MARGIN)
    own = (row_at >= HALO) & (row_at < HALO + OWN) & (place >= MARGIN) & (place < MARGIN + PART)
    shares = [
        jnp.where(edge, 1.0, 0.5)
        for edge in (
            across == 0,
            across == lax.axis_size("au") * OWN - 1,
            along == 0,
            along == lax.axis_size("vert") * 8 * PART - 1,
        )
    ]
    column = jnp.zeros((INNER, LANES), F32)
    upper = (lanes_of((8, LANES)) >= 64).astype(jnp.int32) * count
    walk = zip(slabs(g, INNER, 1, SKIP), slabs(vel, INNER, 1, SKIP), slabs(two, INNER, 1, top))
    for (at, g_mid, g_four, g_two), (_, v_mid, v_four, v_two), (_, x_mid, x_four, x_two) in walk:
        total = jnp.zeros((INNER, LANES), F32)
        for share, g_n, v_n, x_n in zip(shares, g_four, v_four, x_four):
            total = total + (share * g_n) * ((x_n - x_mid) * (v_n - v_mid))
        for other, g_n, v_n, x_n in zip((at, at + 2), g_two, v_two, x_two):
            share = 0.5
            if other == 0:
                share = jnp.where(low, 1.0, 0.5)
            if other == count + 1:
                share = jnp.where(low, 0.5, 1.0)
            total = total + (share * g_n) * ((x_n - x_mid) * (v_n - v_mid))
        total = jnp.where(own, g_mid * total, 0.0)
        column = column + tall(depth_at(upper + at), INNER) * total
        layers[at] = jnp.sum(total.reshape(INNER // 8, 8, LANES), axis=0)
    level = jnp.sum(layers[...], axis=1)

    high = label_window[...] >> 7
    column = jnp.where(low, column + turn(column, 64), 0.0)
    sums = column[HALO - SKIP : HALO - SKIP + OWN, :]
    kind = lax.broadcasted_iota(jnp.int32, (4, LANES), 0)
    left = []
    for at in range(OWN):
        value = jnp.where(high[at : at + 1, :] == kind, sums[at : at + 1, :], 0.0)
        first = value.astype(jnp.bfloat16).astype(F32)
        rest = value - first
        then = rest.astype(jnp.bfloat16).astype(F32)
        left.append(jnp.concatenate([first, then, rest - then, jnp.zeros_like(first)], axis=0).astype(jnp.bfloat16))
    product = lax.dot_general(
        jnp.concatenate(left, axis=1), ones[...], (((1,), (1,)), ((), ())), preferred_element_type=F32
    )
    segments = (product[0:4] + product[4:8]) + product[8:12]

    slot = lanes_of((OWN, LANES)) // PART
    lower = lanes_of((4, LANES)) < 64
    for part in range(8):
        half, at = part // 4, 4 * (part % 4)
        tile = None
        for row in range(4):
            x = two[at + row + 1, TOP + HALO : TOP + HALO + OWN, :]
            x = turn(x, PART * row - (MARGIN - NARROW) - 64 * half)
            tile = x if tile is None else jnp.where(slot == row, x, tile)
        send[part, 0:16, :] = inc[part]
        send[part, 16:32, :] = tile
        here = level[at : at + 4, :]
        here = jnp.where(lower, 0.0, here) if half else jnp.where(lower, here, 0.0)
        send[part, 32:40, :] = jnp.concatenate([segments, here], axis=0)


def sum_kernel(got, spread):
    total = got[0, 32:40, :]
    for source in range(1, 8):
        total = total + got[source, 32:40, :]
    level = jnp.zeros((1, LANES), F32)
    lane = lanes_of((1, LANES))
    for row in range(4):
        level = jnp.where(lane == row, jnp.sum(total[4 + row : 5 + row, :], axis=1, keepdims=True), level)
    pieces = [total[row : row + 1, :] for row in range(4)] + [level]
    line = jnp.concatenate(pieces, axis=1)
    for other in range(spread.shape[0]):
        spread[other] = line


def place_kernel(got, parts, inc, adj, segments, layers):
    lane = lanes_of((OWN, LANES))
    slot = lane // PART
    for out, start in ((inc, 0), (adj, 16)):
        for row in range(4):
            for half in range(2):
                tile = jnp.zeros((OWN, LANES), F32)
                for source in range(4):
                    piece = got[4 * half + source, start : start + 16, :]
                    tile = jnp.where(slot == source, turn(piece, PART * (source - row)), tile)
                out[row, :, half * LANES : (half + 1) * LANES] = tile
    cells = LAYERS * lax.axis_size("au") * OWN * lax.axis_size("vert") * 8 * PART
    total = jnp.sum(parts[...], axis=0)
    lines = [total[:, row * LANES : (row + 1) * LANES] for row in range(4)]
    segments[...] = jnp.concatenate(lines, axis=0) * (1.0 / (cells / NSEG) ** 0.5)
    layers[...] = total[:, 4 * LANES : 4 * LANES + 4] * (1.0 / (cells / LAYERS) ** 0.5)


def shards(velocity, log_visc, labels, seg_dir, layer_dir):
    vert = lax.axis_size("vert")
    across = lax.axis_size("au")
    ahead = [(i, (i + 1) % vert) for i in range(vert)]
    back = [((i + 1) % vert, i) for i in range(vert)]
    upward = [(i, i + 1) for i in range(across - 1)]
    downward = [(i + 1, i) for i in range(across - 1)]
    vmem = pl.BlockSpec(memory_space=pltpu.VMEM)
    hbm = pl.BlockSpec(memory_space=pltpu.HBM)
    label_tile = jax.ShapeDtypeStruct((OWN, LANES), jnp.int32)
    tile, pair, field = sds(OWN, LANES), sds(2, OWN, LANES), sds(4, OWN, 2 * LANES)

    left, right, vel, log = call(
        edge_kernel,
        (pair, pair, field, field),
        [pltpu.SemaphoreType.DMA((2,))],
        in_specs=[hbm] * 2,
        limit=EDGE_LIMIT,
    )(velocity, log_visc)
    from_left = lax.ppermute(right, "vert", ahead)
    from_right = lax.ppermute(left, "vert", back)
    plate, plate_left, plate_right, label_window = call(
        plate_kernel, (sds(OWN, 2 * LANES), tile, tile, label_tile)
    )(labels, seg_dir.reshape(4, LANES))
    plate_before = lax.ppermute(plate_right, "vert", ahead)
    plate_after = lax.ppermute(plate_left, "vert", back)
    send = call(
        window_kernel,
        sds(8, 5, OWN, LANES),
        in_specs=[vmem, vmem, pl.BlockSpec(memory_space=pltpu.SMEM)],
    )(vel, log, layer_dir)
    send = call(patch_kernel, sds(8, 5, OWN, LANES))(send, left, right, from_left, from_right)
    got = lax.all_to_all(send, "row", 0, 0, tiled=True)
    plate_window = call(plate_window_kernel, tile)(plate, plate_left, plate_right, plate_before, plate_after)
    up, down = call(rows_kernel, (sds(62, 8, LANES), sds(62, 8, LANES)))(got, plate_window)
    from_low = lax.ppermute(up, "au", upward)
    from_high = lax.ppermute(down, "au", downward)
    fine = sds(LAYERS, WINDOW, LANES)
    fine_padded = sds(LAYERS + 2, PAD_ROWS, LANES)
    coarse = sds(LAYERS // 2, HALF_TALL, LANES)

    def scratch(layers):
        return (
            [pltpu.VMEM((layers + 2, PAD_ROWS, LANES), F32)] * 3
            + [pltpu.VMEM((layers // 2 + 2, HALF_ROWS, LANES), F32)] * 3
            + [pltpu.VMEM((layers // 2 + 1, WINDOW, LANES), F32)]
        )

    *factors, x_own, f_own, f_up, f_down = call(
        first_kernel,
        (fine_padded, fine, fine, coarse, coarse, coarse, fine_padded)
        + (sds(LAYERS, OWN, LANES), sds(LAYERS // 2, OWN, LANES), sds(25, 8, LANES), sds(25, 8, LANES)),
        [pltpu.VMEM((TILES + 2, WINDOW, LANES), F32)]
        + scratch(LAYERS)
        + [pltpu.VMEM((LAYERS + 2, 8, LANES), F32), pltpu.VMEM((LAYERS // 2 + 2, HALF_ROWS, LANES), F32)],
    )(got, plate_window, from_low, from_high)
    from_low = lax.ppermute(f_up, "au", upward)
    from_high = lax.ppermute(f_down, "au", downward)
    fine = sds(LAYERS // 2, WINDOW, LANES)
    fine_closed = sds(LAYERS // 2 + 2, WINDOW, LANES)
    coarse = sds(LAYERS // 4, HALF_TALL, LANES)
    inc, ones, *factors = call(
        side_kernel,
        (sds(8, OWN, LANES), jax.ShapeDtypeStruct((LANES, OWN * LANES), jnp.bfloat16))
        + (fine_closed, fine, fine, coarse, coarse, coarse, fine_closed),
    )(*factors, x_own, label_window)
    send = call(second_kernel, sds(8, 40, LANES), scratch(LAYERS // 2) + [pltpu.VMEM((LAYERS // 2, 8, LANES), F32)])(
        *factors, f_own, from_low, from_high, inc, label_window, ones
    )
    got = lax.all_to_all(send, "row", 0, 0, tiled=True)
    spread = call(sum_kernel, sds(across * vert, 1, 5 * LANES))(got)
    parts = lax.all_to_all(spread, ("au", "vert"), 0, 0, tiled=True)
    increment, adjoint, hv_segments, hv_layers = call(place_kernel, (field, field, sds(4, LANES), sds(1, 4)))(
        got, parts
    )
    return increment, adjoint, hv_segments.reshape(NSEG), hv_layers.reshape(4)


def solution(mesh):
    in_specs = (P("row", "au", "vert"), P("row", "au", "vert"), P("au", "vert"), P(), P("row"))
    out_specs = (P("row", "au", "vert"), P("row", "au", "vert"), P(), P("row"))
    return jax.shard_map(shards, mesh=mesh, in_specs=in_specs, out_specs=out_specs, check_vma=False)
```
